256 devices in a mesh: inst: 4 (over z_lo), ctx: 16 (over z_hi, x, core), tp: 4 (over y).
Axes of the slice: x: 4, y: 4, z: 8 (z_hi: 2, z_lo: 4; z = z_hi * 4 + z_lo), core: 2. Of those that a mesh axis runs over, the one named last changes fastest.
Arguments:
- queries: bfloat16 [8192, 8192], P(('inst', 'ctx'), 'tp'), may hold values from -420 to 420
- suffix_kv: bfloat16 [2, 8192, 1024], P(None, ('inst', 'ctx'), 'tp'), may hold values from -6 to 6
- pool: bfloat16 [1024, 2, 128, 1024], P(('inst', 'ctx'), None, 'tp'), may hold values from -6 to 6
- hits: int32 [4, 3, 64], replicated, may hold values from -1 to 1023, as said below
- lengths: int32 [4, 3], replicated, may hold values from 1 to 9, 16 in all within a row
- write_slot: int32 [64, 16], P(('inst', 'ctx')), may hold values from 0 to 15, each once within a row
Outputs:
- attended: bfloat16 [8192, 8192], P(('inst', 'ctx'), 'tp')
- new_pool: bfloat16 [1024, 2, 128, 1024], P(('inst', 'ctx'), None, 'tp')
The draws below stay inside these ranges and needn't reach their ends.
Inputs may be any that keep to these rules, and one draw needn't show every extreme that they name: hits[i, r, o] is either -1 or a block id from o * 16 to o * 16 + 16 - 1 (owner o is device o of inst+ctx, inst slowest); for every instance i and owner o exactly one request r has an id. `write_slot`: each row is a permutation.
All inputs are finite; a program needn't handle non-finite values.
Results may differ from the reference program's by a relative error of at most 0.009.
Values may be sent and summed in bfloat16 or wider, within the bound.
No kernel may reach another device: no remote copies, remote signals or barrier semaphores. Data moves between devices by JAX's collectives and lax.ppermute only.
A program may use at most 128 MiB of HBM per device.

```python
import math
import jax
import jax.numpy as jnp
import numpy as np
from jax import lax

HQ = 64
KVH = 8
HD = 128
BLOCK = 128
REQS = 3
BLK_DEV = 16
TOK_DEV = 128
TOK_INST = 2048
TOKENS = 8192
OWNERS = 64
BLOCKS = 1024
UNITS = 16
N_INST = 4
N_CTX = 16


def draw_queries(key, part):
    key = jax.random.fold_in(key, 5)
    first = jax.random.fold_in(key, 0)
    shape = (TOKENS, HQ * HD)
    values = jnp.clip(jax.random.normal(first, shape, jnp.float32), -6.0, 6.0)
    return values.astype(jnp.bfloat16)


def draw_hits(key, part):
    key = jax.random.fold_in(key, 11)
    first, second = jax.random.split(key)
    chosen = jax.random.randint(first, (N_INST, OWNERS), 0, REQS)
    slots = jax.random.randint(second, (N_INST, OWNERS), 0, BLK_DEV)
    corner = (jnp.arange(N_INST)[:, None] == 0) & (jnp.arange(OWNERS)[None, :] == OWNERS - 1)
    slots = jnp.where(corner, BLK_DEV - 1, slots)
    block_ids = jnp.arange(OWNERS)[None, :] * BLK_DEV + slots
    picked = chosen[:, None, :] == jnp.arange(REQS)[None, :, None]
    return jnp.where(picked, block_ids[:, None, :], -1).astype(jnp.int32)


def shard_levels(own_key, dims, cuts, least, largest):
    def one(axis_at, parts):
        draws = jax.random.uniform(jax.random.fold_in(jax.random.fold_in(own_key, 6), axis_at), (parts,), jnp.float32, least / len(cuts), largest / len(cuts))
        return jnp.repeat(jnp.exp(draws), dims[axis_at] // parts).reshape((-1,) + (1,) * (len(dims) - axis_at - 1))

    gain = one(*cuts[0])
    for cut in cuts[1:]:
        gain = gain * one(*cut)
    return gain


def length_profile(number_of, total, most, slope):
    loads = [(1 << 20) // math.isqrt(standing ** slope) + 1 for standing in range(2, number_of + 1)]
    spare, given = total - most - (number_of - 1), [1] * (number_of - 1)
    while spare > 0:
        free = [i for i in range(number_of - 1) if given[i] < most]
        whole, left = sum([loads[i] for i in free]), spare
        for i in free:
            extra = min(most - given[i], max(1, left * loads[i] // whole), spare)
            given[i] = given[i] + extra
            spare = spare - extra
    return np.array([most] + given)


def ragged_sizes(stream_key, amount, total, reach, lean):
    if amount == 2:
        one = jax.random.randint(stream_key, (), max(1, total - reach), min(reach, total - 1) + 1)
        return jnp.stack([one, total - one])
    sizes = jnp.asarray(length_profile(amount, total, reach, lean), jnp.int32)
    couples = (amount - 1) // 2
    giver, taker = sizes[1:1 + 2 * couples:2], sizes[2:2 + 2 * couples:2]
    slack = jnp.minimum(giver - 1, reach - taker)
    moved = jax.random.randint(jax.random.fold_in(stream_key, 1), (couples,), 0, 1 << 20) % (slack + 1)
    sizes = sizes.at[1:1 + 2 * couples:2].set(giver - moved).at[2:2 + 2 * couples:2].set(taker + moved)
    return sizes[jax.random.permutation(jax.random.fold_in(stream_key, 2), amount)]


def bell_draw(stream_key, dims, width, reach, cuts=(), held_as=jnp.bfloat16):
    values = jax.random.normal(stream_key, dims, jnp.float32) * width
    if len(cuts) > 0:
        values = shard_levels(stream_key, dims, cuts, -0.22, 0.18) * values
    return jnp.clip(values, min=-reach, max=reach).astype(held_as)


def setup_inputs(seed: int = 0) -> dict:
    streams_of = jax.random.split(jax.random.key(seed), 7)
    return {
        "queries": draw_queries(jax.random.fold_in(streams_of[6], 71), 0),
        "suffix_kv": bell_draw(streams_of[1], (2, TOKENS, KVH * HD), 1.0, 6.0, ((1, 64), (2, 4))),
        "pool": bell_draw(streams_of[2], (BLOCKS, 2, BLOCK, KVH * HD), 1.0, 6.0, ((0, 64), (2, 4))),
        "hits": draw_hits(jax.random.fold_in(streams_of[6], 71), 0),
        "lengths": jax.vmap(lambda own: ragged_sizes(own, REQS, UNITS, max(1, UNITS - 3 - UNITS // 4), 2))(jax.random.split(streams_of[4], N_INST)).reshape((N_INST, REQS)).astype(jnp.int32),
        "write_slot": jax.vmap(lambda own: jax.random.permutation(own, BLK_DEV))(jax.random.split(streams_of[5], OWNERS)).reshape((OWNERS, BLK_DEV)).astype(jnp.int32),
    }


NEG_FILL = -1e30


def request_of(positions, boundaries):
    return jnp.sum((positions[:, None] >= boundaries[None, :]).astype(jnp.int32), axis=1).astype(jnp.int32)


def attend_block(query_block, key_rows, value_rows, allowed):
    scale = HD ** -0.5

    def one_head(operands):
        query_head, key_head, value_head = operands
        scores = jnp.einsum("qgd,kd->qgk", query_head.astype(jnp.float32), key_head.astype(jnp.float32)) * scale
        visible = allowed[:, None, :]
        scores = jnp.where(visible, scores, NEG_FILL)
        highest = jnp.max(scores, axis=-1, keepdims=True)
        weights = jnp.where(visible, jnp.exp(scores - highest), 0.0)
        totals = jnp.sum(weights, axis=-1, keepdims=True)
        rounded = lax.optimization_barrier(weights.astype(jnp.bfloat16)).astype(jnp.float32)
        return jnp.einsum("qgk,kd->qgd", rounded, value_head.astype(jnp.float32)) / totals

    heads_out = lax.map(one_head, (jnp.transpose(query_block, (1, 0, 2, 3)), jnp.transpose(key_rows, (1, 0, 2)), jnp.transpose(value_rows, (1, 0, 2))))
    return jnp.transpose(heads_out, (1, 0, 2, 3))


def reference(queries, suffix_kv, pool, hits, lengths, write_slot):
    group_size = HQ // KVH
    query_rows = math.gcd(TOK_INST, 512)
    block_total = TOK_INST // query_rows
    positions = jnp.arange(TOK_INST, dtype=jnp.int32)
    pieces = []
    for instance in range(N_INST):
        boundaries = (jnp.cumsum(lengths[instance]) * BLOCK).astype(jnp.int32)
        suffix_req = request_of(positions, boundaries)
        chosen = hits[instance]
        block_ids = jnp.max(chosen, axis=0).astype(jnp.int32)
        owner_req = jnp.sum(jnp.where(chosen >= 0, jnp.arange(REQS, dtype=jnp.int32)[:, None], 0), axis=0).astype(jnp.int32)
        prefix = jnp.take(pool, block_ids, axis=0)
        suffix = suffix_kv[:, instance * TOK_INST:(instance + 1) * TOK_INST]
        key_rows = jnp.concatenate([prefix[:, 0].reshape(OWNERS * BLOCK, KVH, HD), suffix[0].reshape(TOK_INST, KVH, HD)], axis=0)
        value_rows = jnp.concatenate([prefix[:, 1].reshape(OWNERS * BLOCK, KVH, HD), suffix[1].reshape(TOK_INST, KVH, HD)], axis=0)
        key_req = jnp.concatenate([jnp.repeat(owner_req, BLOCK), suffix_req]).astype(jnp.int32)
        key_pos = jnp.concatenate([jnp.full((OWNERS * BLOCK,), -1, jnp.int32), positions])
        query_blocks = queries[instance * TOK_INST:(instance + 1) * TOK_INST].reshape(block_total, query_rows, KVH, group_size, HD)
        starts = jnp.arange(block_total, dtype=jnp.int32) * query_rows

        def one_block(operands):
            query_block, first_row = operands
            query_pos = first_row + jnp.arange(query_rows, dtype=jnp.int32)
            query_req = request_of(query_pos, boundaries)
            allowed = (key_req[None, :] == query_req[:, None]) & (key_pos[None, :] <= query_pos[:, None])
            return attend_block(query_block, key_rows, value_rows, allowed)

        result = lax.map(one_block, (query_blocks, starts))
        pieces.append(result.reshape(TOK_INST, HQ * HD).astype(jnp.bfloat16))
    attended = jnp.concatenate(pieces, axis=0)
    block_count = TOK_DEV // BLOCK
    written = suffix_kv.reshape(2, N_INST, N_CTX, block_count, BLOCK, KVH * HD)
    written = jnp.transpose(written, (1, 2, 3, 0, 4, 5))
    incoming = jnp.roll(written, 1, axis=0)
    shaped = pool.reshape(N_INST, N_CTX, BLK_DEV, 2, BLOCK, KVH * HD)
    slots = write_slot.reshape(N_INST, N_CTX, BLK_DEV)
    local_ids = jnp.arange(BLK_DEV, dtype=jnp.int32)
    for column in range(block_count):
        target = slots[:, :, column][:, :, None] == local_ids[None, None, :]
        shaped = jnp.where(target[:, :, :, None, None, None], incoming[:, :, column][:, :, None], shaped)
    new_pool = shaped.reshape(BLOCKS, 2, BLOCK, KVH * HD)
    return attended, new_pool
```

```python
import functools
import math

import jax
import jax.numpy as jnp
from jax import lax
from jax.experimental import pallas as pl
from jax.experimental.pallas import tpu as pltpu
from jax.sharding import Mesh, PartitionSpec as P

HD = 128
BLOCK = 128
TILE = 256
NEG = -1e30
SCALE = HD ** -0.5 * math.log2(math.e)
VMEM_LIMIT = 48 * 1024 * 1024


def shifted(block, axis, distance):
    count = lax.axis_size(axis)
    return lax.ppermute(block, axis, [(i, (i + distance) % count) for i in range(count)])


def request_of(positions, boundaries):
    return jnp.sum((positions[..., None] >= boundaries).astype(jnp.int32), axis=-1)


def pick_kernel(slot_ref, block_ref, out_ref):
    for part in range(8):
        out_ref[0, part % 2, part // 2] = block_ref[0, :, :, part * HD : (part + 1) * HD]


def pick_blocks(slots, pool):
    insts = slots.shape[0]
    _, two, rows, cols = pool.shape
    return pl.pallas_call(
        pick_kernel,
        grid_spec=pltpu.PrefetchScalarGridSpec(
            num_scalar_prefetch=1,
            grid=(insts,),
            in_specs=[pl.BlockSpec((1, two, rows, cols), lambda i, s: (s[i], 0, 0, 0))],
            out_specs=pl.BlockSpec((1, 2, 4, two, rows, HD), lambda i, s: (i, 0, 0, 0, 0, 0)),
        ),
        out_shape=jax.ShapeDtypeStruct((insts, 2, 4, two, rows, HD), pool.dtype),
        name="pick_blocks",
    )(slots, pool)


def step(unit, keys, values, queries_ref, high_ref, total_ref, acc_ref):
    for tile in range(queries_ref.shape[2] // TILE):
        lanes = slice(tile * TILE, (tile + 1) * TILE)
        scores = SCALE * jnp.dot(
            keys, queries_ref[unit, :, lanes], preferred_element_type=jnp.float32
        )
        before = high_ref[unit, :, lanes]
        high = jnp.maximum(before, jnp.max(scores, axis=0, keepdims=True))
        faded = jnp.exp2(before - high)
        weights = jnp.exp2(scores - high)
        high_ref[unit, :, lanes] = high
        total_ref[unit, :, lanes] = total_ref[unit, :, lanes] * faded + jnp.sum(
            weights, axis=0, keepdims=True
        )
        summed = lax.dot_general(
            values,
            weights.astype(jnp.bfloat16),
            (((0,), (0,)), ((), ())),
            preferred_element_type=jnp.float32,
        )
        acc_ref[unit, :, lanes] = acc_ref[unit, :, lanes] * faded + summed


def first_step(unit, keys, values, queries_ref, high_ref, total_ref, acc_ref):
    for tile in range(queries_ref.shape[2] // TILE):
        lanes = slice(tile * TILE, (tile + 1) * TILE)
        scores = SCALE * jnp.dot(
            keys, queries_ref[unit, :, lanes], preferred_element_type=jnp.float32
        )
        key_at = lax.broadcasted_iota(jnp.int32, scores.shape, 0)
        query_at = lax.rem(lax.broadcasted_iota(jnp.int32, scores.shape, 1), BLOCK)
        scores = jnp.where(key_at <= query_at, scores, NEG)
        high = jnp.max(scores, axis=0, keepdims=True)
        weights = jnp.exp2(scores - high)
        high_ref[unit, :, lanes] = high
        total_ref[unit, :, lanes] = jnp.sum(weights, axis=0, keepdims=True)
        acc_ref[unit, :, lanes] = lax.dot_general(
            values,
            weights.astype(jnp.bfloat16),
            (((0,), (0,)), ((), ())),
            preferred_element_type=jnp.float32,
        )


def sweep(need_ref, load, block_count, keys_ref, values_ref, state):
    for unit in range(2):
        count = jnp.int32(0)
        for block in range(block_count):
            wanted = need_ref[unit, block]

            @pl.when(wanted > 0)
            def _(count=count, block=block):
                keys, values = load(block)
                rows = pl.ds(pl.multiple_of(count * BLOCK, BLOCK), BLOCK)
                keys_ref[rows, :] = keys
                values_ref[rows, :] = values

            count = count + wanted

        def pair(turn, carry, unit=unit):
            rows = pl.ds(pl.multiple_of(turn * 2 * BLOCK, 2 * BLOCK), 2 * BLOCK)
            step(unit, keys_ref[rows, :], values_ref[rows, :], *state)
            return carry

        lax.fori_loop(0, count // 2, pair, 0)

        @pl.when(count % 2 > 0)
        def _(count=count, unit=unit):
            rows = pl.ds(pl.multiple_of((count - 1) * BLOCK, BLOCK), BLOCK)
            step(unit, keys_ref[rows, :], values_ref[rows, :], *state)


def suffix_kernel(need_ref, mine_ref, other_ref, *refs):
    chunks, refs = refs[:4], refs[4:]
    queries_ref, high_ref, total_ref, acc_ref, keys_ref, values_ref = refs
    state = (queries_ref, high_ref, total_ref, acc_ref)
    for unit, source in enumerate((mine_ref, other_ref)):
        for head in range(source.shape[1] // HD):
            cols = slice(head * HD, (head + 1) * HD)
            queries_ref[unit, :, cols] = source[:, cols].T
        first_step(unit, chunks[0][0, unit, 0], chunks[0][0, unit, 1], *state)

    def load(block):
        chunk, half, unit = chunks[block // 4], block // 2 % 2, block % 2
        return chunk[half, unit, 0], chunk[half, unit, 1]

    sweep(need_ref, load, 16, keys_ref, values_ref, state)


def loader(chunks):
    def load(block):
        chunk, place = chunks[block // 8], block % 8
        rows = (BLOCK, HD)
        return chunk[place, :, 0].reshape(rows), chunk[place, :, 1].reshape(rows)

    return load


def prefix_kernel(chunk_count, last, need_ref, queries_ref, high_in, total_in, acc_in, *refs):
    chunks, refs = refs[:chunk_count], refs[chunk_count:]
    if last:
        out_ref, high_ref, total_ref, acc_ref, keys_ref, values_ref = refs
    else:
        high_ref, total_ref, acc_ref, keys_ref, values_ref = refs
    high_ref[...] = high_in[...]
    total_ref[...] = total_in[...]
    acc_ref[...] = acc_in[...]
    state = (queries_ref, high_ref, total_ref, acc_ref)
    sweep(need_ref, loader(chunks), 8 * chunk_count, keys_ref, values_ref, state)
    if last:
        for unit in range(2):
            for head in range(out_ref.shape[2] // HD):
                cols = slice(head * HD, (head + 1) * HD)
                done = acc_ref[unit, :, cols] / total_ref[unit, :, cols]
                out_ref[unit, :, cols] = done.T.astype(out_ref.dtype)


SMEM = pl.BlockSpec(memory_space=pltpu.SMEM)
VMEM = pl.BlockSpec(memory_space=pltpu.VMEM)


def scratch(block_count):
    return [pltpu.VMEM((block_count * BLOCK, HD), jnp.bfloat16)] * 2


def cost(block_count, rows):
    flops = 4 * block_count // 3 * BLOCK * HD * rows
    return pl.CostEstimate(flops=flops, bytes_accessed=4 << 20, transcendentals=0)


def state_shapes(rows):
    return [
        jax.ShapeDtypeStruct((2, 1, rows), jnp.float32),
        jax.ShapeDtypeStruct((2, 1, rows), jnp.float32),
        jax.ShapeDtypeStruct((2, HD, rows), jnp.float32),
    ]


def suffix_attention(need, mine, other, chunks):
    rows = mine.shape[1]
    return pl.pallas_call(
        suffix_kernel,
        in_specs=[SMEM] + [VMEM] * 6,
        out_specs=[VMEM] * 4,
        out_shape=[jax.ShapeDtypeStruct((2, HD, rows), jnp.bfloat16)] + state_shapes(rows),
        scratch_shapes=scratch(16),
        compiler_params=pltpu.CompilerParams(vmem_limit_bytes=VMEM_LIMIT),
        cost_estimate=cost(16, 2 * rows),
        name="suffix_attention",
    )(need, mine, other, *chunks)


def prefix_attention(need, state, chunks, last):
    rows = state[0].shape[2]
    count = len(chunks)
    shapes = state_shapes(rows)
    if last:
        out_shape = [jax.ShapeDtypeStruct((2, BLOCK, rows), jnp.bfloat16)]
        extra = [pltpu.VMEM(shape.shape, shape.dtype) for shape in shapes]
    else:
        out_shape, extra = shapes, []
    return pl.pallas_call(
        functools.partial(prefix_kernel, count, last),
        in_specs=[SMEM] + [VMEM] * (4 + count),
        out_specs=[VMEM] * len(out_shape),
        out_shape=out_shape,
        scratch_shapes=extra + scratch(8 * count),
        compiler_params=pltpu.CompilerParams(vmem_limit_bytes=VMEM_LIMIT),
        cost_estimate=cost(8 * count, 2 * rows),
        name="prefix_attention",
    )(need, *state, *chunks)


def halves(array, core, axis):
    first, second = jnp.split(array, 2, axis=axis)
    return jnp.where(core == 0, first, second), jnp.where(core == 0, second, first)


def local(queries, suffix_kv, pool, hits, lengths, write_slot):
    inst, zh, x, core = (lax.axis_index(name) for name in ("inst", "zh", "x", "core"))
    owner = ((inst * 2 + zh) * 4 + x) * 2 + core
    blk_count = pool.shape[0]
    part_rows = pool.shape[2]

    mine_hits = lax.dynamic_index_in_dim(hits, owner, axis=2, keepdims=False)
    slots = jnp.max(mine_hits, axis=1) - owner * blk_count
    sent = pick_blocks(slots, pool).reshape(32, 2, part_rows, HD)
    fetched = lax.all_to_all(sent, ("inst", "core", "tp"), split_axis=0, concat_axis=0, tiled=True)
    own = fetched.reshape(8, 4, 2, part_rows, HD)

    query_mine, query_sent = halves(queries, core, 1)
    query_other = shifted(query_sent, "core", 1)
    suffix_mine, suffix_sent = halves(suffix_kv, core, 2)
    suffix_other = shifted(suffix_sent, "core", 1)
    suffix_own = jnp.stack([suffix_mine, suffix_other])
    suffix_own = jnp.stack([suffix_own, shifted(suffix_own, "zh", 1)])
    suffix_chunks = [suffix_own] + [shifted(suffix_own, "x", far) for far in (1, 3, 2)]

    boundaries = jnp.cumsum(lax.dynamic_index_in_dim(lengths, inst, axis=0, keepdims=False))
    units = (zh * 4 + x) * 2 + jnp.stack([core, 1 - core])
    unit_req = request_of(units, boundaries)
    back = jnp.array([0, 1, 3, 2], jnp.int32)
    from_x = lax.rem(x - back + 4, 4)
    from_zh = jnp.stack([zh, 1 - zh])
    from_unit = jnp.stack([core, 1 - core])
    at = (from_zh[None, :, None] * 4 + from_x[:, None, None]) * 2 + from_unit[None, None, :]
    at = at.reshape(1, 16)
    suffix_need = (
        (request_of(at, boundaries) == unit_req[:, None]) & (at < units[:, None])
    ).astype(jnp.int32)

    chosen = lax.dynamic_index_in_dim(hits, inst, axis=0, keepdims=False)
    owner_req = jnp.sum(
        jnp.where(chosen >= 0, jnp.arange(chosen.shape[0], dtype=jnp.int32)[:, None], 0), axis=0
    )
    need_all = (owner_req[None, :] == unit_req[:, None]).astype(jnp.int32)
    need_all = jnp.transpose(need_all.reshape(2, 4, 2, 4, 2), (0, 2, 3, 1, 4)).reshape(2, 2, 4, 8)

    def prefix_need(half):
        rows = lax.dynamic_index_in_dim(need_all, half, axis=1, keepdims=False)
        return jnp.take(rows, from_x, axis=1).reshape(2, 32)

    state = suffix_attention(suffix_need, query_mine, query_other, suffix_chunks)
    queries_t = state[0]
    across = shifted(own, "zh", 1)
    chunks = [own] + [shifted(own, "x", far) for far in (1, 3, 2)]
    state = prefix_attention(prefix_need(zh), state, chunks, False)
    chunks = [across] + [shifted(across, "x", far) for far in (1, 3, 2)]
    done = prefix_attention(prefix_need(1 - zh), [queries_t] + list(state), chunks, True)[0]
    theirs = shifted(done[1], "core", 1)
    first = jnp.where(core == 0, done[0], theirs)
    second = jnp.where(core == 0, theirs, done[0])
    attended = jnp.concatenate([first, second], axis=1)

    layout = suffix_kv.reshape(2, 4, part_rows, suffix_kv.shape[2])
    layout = lax.all_to_all(layout, "tp", split_axis=1, concat_axis=1, tiled=True)
    incoming = jnp.transpose(layout, (0, 2, 1, 3)).reshape(1, 2, part_rows, pool.shape[3])
    incoming = shifted(incoming, "inst", 1)
    new_pool = lax.dynamic_update_slice(pool, incoming, (write_slot[0, 0], 0, 0, 0))
    return attended, new_pool


def solution(mesh):
    split = Mesh(mesh.devices.reshape(4, 2, 4, 2, 4), ("inst", "zh", "x", "core", "tp"))
    ctx = ("inst", "zh", "x", "core")
    placed = (
        P(ctx, "tp"),
        P(None, ctx, "tp"),
        P(ctx, None, "tp", None),
        P(),
        P(),
        P(ctx, None),
    )
    return jax.shard_map(
        local,
        mesh=split,
        in_specs=placed,
        out_specs=(P(ctx, "tp"), P(ctx, None, "tp", None)),
        check_vma=False,
    )
```

```python
import functools
import math

import jax
import jax.numpy as jnp
from jax import lax
from jax.experimental import pallas as pl
from jax.experimental.pallas import tpu as pltpu
from jax.sharding import Mesh, PartitionSpec as P

HD = 128
BLOCK = 128
NEG = -1e30
SCALE = HD ** -0.5 * math.log2(math.e)
VMEM_LIMIT = 48 * 1024 * 1024


def shifted(block, axis, distance):
    count = lax.axis_size(axis)
    return lax.ppermute(block, axis, [(i, (i + distance) % count) for i in range(count)])


def pick_kernel(slot_ref, block_ref, out_ref):
    for part in range(8):
        out_ref[0, part % 2, part // 2] = block_ref[0, :, :, part * HD : (part + 1) * HD]


def pick_blocks(slots, pool):
    insts = slots.shape[0]
    _, two, rows, cols = pool.shape
    return pl.pallas_call(
        pick_kernel,
        grid_spec=pltpu.PrefetchScalarGridSpec(
            num_scalar_prefetch=1,
            grid=(insts,),
            in_specs=[pl.BlockSpec((1, two, rows, cols), lambda i, s: (s[i], 0, 0, 0))],
            out_specs=pl.BlockSpec((1, 2, 4, two, rows, HD), lambda i, s: (i, 0, 0, 0, 0, 0)),
        ),
        out_shape=jax.ShapeDtypeStruct((insts, 2, 4, two, rows, HD), pool.dtype),
        name="pick_blocks",
    )(slots, pool)


def step(unit, keys, values, queries_ref, high_ref, total_ref, acc_ref):
    scores = SCALE * jnp.dot(keys, queries_ref[unit], preferred_element_type=jnp.float32)
    before = high_ref[unit]
    high = jnp.maximum(before, jnp.max(scores, axis=0, keepdims=True))
    faded = jnp.exp2(before - high)
    weights = jnp.exp2(scores - high)
    high_ref[unit] = high
    total_ref[unit] = total_ref[unit] * faded + jnp.sum(weights, axis=0, keepdims=True)
    summed = jnp.dot(values, weights.astype(jnp.bfloat16), preferred_element_type=jnp.float32)
    acc_ref[unit] = acc_ref[unit] * faded + summed


def first_step(unit, keys, values, queries_ref, high_ref, total_ref, acc_ref):
    scores = SCALE * jnp.dot(keys, queries_ref[unit], preferred_element_type=jnp.float32)
    key_at = lax.broadcasted_iota(jnp.int32, scores.shape, 0)
    query_at = lax.rem(lax.broadcasted_iota(jnp.int32, scores.shape, 1), BLOCK)
    scores = jnp.where(key_at <= query_at, scores, NEG)
    high = jnp.max(scores, axis=0, keepdims=True)
    weights = jnp.exp2(scores - high)
    high_ref[unit] = high
    total_ref[unit] = jnp.sum(weights, axis=0, keepdims=True)
    acc_ref[unit] = jnp.dot(
        values.T, weights.astype(jnp.bfloat16), preferred_element_type=jnp.float32
    )


def sweep(wanted_of, loads, keys_ref, values_ref, state):
    for unit in range(2):
        count = jnp.int32(0)
        for place, load in enumerate(loads):
            wanted = wanted_of(unit, place)

            @pl.when(wanted)
            def _(count=count, load=load):
                keys, values = load()
                span = pl.ds(pl.multiple_of(count * BLOCK, BLOCK), BLOCK)
                keys_ref[span, :] = keys
                values_ref[:, span] = values.T

            count = count + wanted.astype(jnp.int32)

        def many(first, blocks, unit=unit):
            span = pl.ds(pl.multiple_of(first * BLOCK, BLOCK), blocks * BLOCK)
            step(unit, keys_ref[span, :], values_ref[:, span], *state)

        def turn(index, carry, many=many):
            many(index * 4, 4)
            return carry

        lax.fori_loop(0, count // 4, turn, 0)

        @pl.when(count % 4 >= 2)
        def _(count=count, many=many):
            many(count // 4 * 4, 2)

        @pl.when(count % 2 > 0)
        def _(count=count, many=many):
            many(count - 1, 1)


def unit_places(coords_ref):
    zh, x, core = coords_ref[1], coords_ref[2], coords_ref[3]
    return (zh * 4 + x) * 2 + core, ((1 - zh) * 4 + x) * 2 + core


def request_at(lengths_ref, inst, place):
    first = lengths_ref[inst, 0]
    second = first + lengths_ref[inst, 1]
    third = second + lengths_ref[inst, 2]
    return sum((place >= edge).astype(jnp.int32) for edge in (first, second, third))


def suffix_kernel(coords_ref, lengths_ref, mine_ref, other_ref, near_ref, far_ref, *refs):
    queries_ref, high_ref, total_ref, acc_ref, keys_ref, values_ref = refs
    state = (queries_ref, high_ref, total_ref, acc_ref)
    for unit, source in enumerate((mine_ref, other_ref)):
        for head in range(source.shape[1] // HD):
            cols = slice(head * HD, (head + 1) * HD)
            queries_ref[unit, :, cols] = source[:, cols].T
        first_step(unit, near_ref[0, unit, 0], near_ref[0, unit, 1], *state)
    inst, zh, x, core = (coords_ref[i] for i in range(4))
    units = unit_places(coords_ref)
    unit_reqs = [request_at(lengths_ref, inst, place) for place in units]
    loads, places = [], []
    for turned, source in enumerate((near_ref, far_ref)):
        for back in range(4):
            for side in range(2):
                loads.append(lambda s=source, b=back, h=side: (s[b, h, 0], s[b, h, 1]))
                from_zh = 1 - zh if side else zh
                from_core = 1 - core if turned else core
                places.append((from_zh * 4 + lax.rem(x - back + 4, 4)) * 2 + from_core)
    reqs = [request_at(lengths_ref, inst, place) for place in places]

    def wanted_of(unit, index):
        return (places[index] < units[unit]) & (reqs[index] == unit_reqs[unit])

    sweep(wanted_of, loads, keys_ref, values_ref, state)


def prefix_kernel(origins, last, coords_ref, lengths_ref, hits_ref, queries_ref, *refs):
    high_in, total_in, acc_in, refs = refs[0], refs[1], refs[2], refs[3:]
    chunks, refs = refs[: len(origins)], refs[len(origins) :]
    if last:
        out_ref, high_ref, total_ref, acc_ref, keys_ref, values_ref = refs
    else:
        high_ref, total_ref, acc_ref, keys_ref, values_ref = refs
    high_ref[...] = high_in[...]
    total_ref[...] = total_in[...]
    acc_ref[...] = acc_in[...]
    state = (queries_ref, high_ref, total_ref, acc_ref)
    inst, _, x, core = (coords_ref[i] for i in range(4))
    reqs = [request_at(lengths_ref, inst, place) for place in unit_places(coords_ref)]
    loads, owners = [], []
    for chunk, (back, turned, first) in zip(chunks, origins):
        from_x = lax.rem(x - back + 4, 4)
        from_core = 1 - core if turned else core
        for place in range(chunk.shape[0]):

            def load(chunk=chunk, place=place):
                shape = (BLOCK, HD)
                return chunk[place, :, 0].reshape(shape), chunk[place, :, 1].reshape(shape)

            loads.append(load)
            owners.append((first + place) * 8 + from_x * 2 + from_core)

    def wanted_of(unit, index):
        return hits_ref[inst, reqs[unit], owners[index]] >= 0

    sweep(wanted_of, loads, keys_ref, values_ref, state)
    if last:
        for unit in range(2):
            for head in range(out_ref.shape[2] // HD):
                cols = slice(head * HD, (head + 1) * HD)
                done = acc_ref[unit, :, cols] / total_ref[unit, :, cols]
                out_ref[unit, :, cols] = done.T.astype(out_ref.dtype)


def write_kernel(slot_ref, pool_ref, block_ref, out_ref, sems):
    copies = [
        pltpu.make_async_copy(pool_ref.at[place], out_ref.at[place], sems.at[place])
        for place in range(pool_ref.shape[0])
    ]
    for place, copy in enumerate(copies):
        pl.when(slot_ref[0, 0] != place)(copy.start)
    arrived = pltpu.make_async_copy(
        block_ref, out_ref.at[slot_ref[0, 0]], sems.at[pool_ref.shape[0]]
    )
    arrived.start()
    for place, copy in enumerate(copies):
        pl.when(slot_ref[0, 0] != place)(copy.wait)
    arrived.wait()


def write_block(slots, pool, block):
    return pl.pallas_call(
        write_kernel,
        in_specs=[SMEM, pl.BlockSpec(memory_space=pl.ANY), VMEM],
        out_specs=pl.BlockSpec(memory_space=pl.ANY),
        out_shape=jax.ShapeDtypeStruct(pool.shape, pool.dtype),
        scratch_shapes=[pltpu.SemaphoreType.DMA((pool.shape[0] + 1,))],
        cost_estimate=pl.CostEstimate(flops=0, bytes_accessed=2 * pool.size * 2, transcendentals=0),
        name="write_block",
    )(slots, pool, block)


SMEM = pl.BlockSpec(memory_space=pltpu.SMEM)
VMEM = pl.BlockSpec(memory_space=pltpu.VMEM)


def scratch(block_count):
    return [
        pltpu.VMEM((block_count * BLOCK, HD), jnp.bfloat16),
        pltpu.VMEM((HD, block_count * BLOCK), jnp.bfloat16),
    ]


def cost(block_count, rows):
    flops = 4 * block_count * BLOCK * HD * rows
    return pl.CostEstimate(flops=flops, bytes_accessed=4 << 20, transcendentals=0)


def state_shapes(rows):
    return [
        jax.ShapeDtypeStruct((2, 1, rows), jnp.float32),
        jax.ShapeDtypeStruct((2, 1, rows), jnp.float32),
        jax.ShapeDtypeStruct((2, HD, rows), jnp.float32),
    ]


def suffix_attention(coords, lengths, mine, other, near, far):
    rows = mine.shape[1]
    return pl.pallas_call(
        suffix_kernel,
        in_specs=[SMEM] * 2 + [VMEM] * 4,
        out_specs=[VMEM] * 4,
        out_shape=[jax.ShapeDtypeStruct((2, HD, rows), jnp.bfloat16)] + state_shapes(rows),
        scratch_shapes=scratch(16),
        compiler_params=pltpu.CompilerParams(vmem_limit_bytes=VMEM_LIMIT),
        cost_estimate=cost(8, 2 * rows),
        name="suffix_attention",
    )(coords, lengths, mine, other, near, far)


def prefix_attention(where, queries_t, state, chunks, last=False):
    rows = queries_t.shape[2]
    arrays = [chunk for chunk, _ in chunks]
    block_count = sum(array.shape[0] for array in arrays)
    shapes = state_shapes(rows)
    if last:
        out_shape = [jax.ShapeDtypeStruct((2, BLOCK, rows), jnp.bfloat16)]
        extra = [pltpu.VMEM(shape.shape, shape.dtype) for shape in shapes]
    else:
        out_shape, extra = shapes, []
    return pl.pallas_call(
        functools.partial(prefix_kernel, [origin for _, origin in chunks], last),
        in_specs=[SMEM] * 3 + [VMEM] * (4 + len(arrays)),
        out_specs=[VMEM] * len(out_shape),
        out_shape=out_shape,
        scratch_shapes=extra + scratch(block_count),
        compiler_params=pltpu.CompilerParams(vmem_limit_bytes=VMEM_LIMIT),
        cost_estimate=cost(block_count, 2 * rows),
        name="prefix_attention",
    )(*where, queries_t, *state, *arrays)


def halves(array, side, axis):
    first, second = jnp.split(array, 2, axis=axis)
    return jnp.where(side == 0, first, second), jnp.where(side == 0, second, first)


def local(queries, suffix_kv, pool, hits, lengths, write_slot):
    coords = [lax.axis_index(name) for name in ("inst", "zh", "x", "core")]
    inst, zh, x, core = coords
    owner = ((inst * 2 + zh) * 4 + x) * 2 + core
    coords = jnp.stack(coords).astype(jnp.int32)
    blk_count = pool.shape[0]
    part_rows = pool.shape[2]

    mine_hits = lax.dynamic_index_in_dim(hits, owner, axis=2, keepdims=False)
    slots = jnp.max(mine_hits, axis=1) - owner * blk_count
    sent = pick_blocks(slots, pool).reshape(32, 2, part_rows, HD)
    fetched = lax.all_to_all(sent, ("inst", "zh", "tp"), split_axis=0, concat_axis=0, tiled=True)

    suffix_mine, suffix_sent = halves(suffix_kv, zh, 2)
    near = jnp.stack([suffix_mine, shifted(suffix_sent, "zh", 1)])
    near = jnp.stack([near] + [shifted(near, "x", far) for far in (1, 2, 3)])
    far = shifted(near, "core", 1)

    queries, fetched = lax.optimization_barrier((queries, fetched))
    own = fetched.reshape(8, 4, 2, part_rows, HD)
    query_mine, query_sent = halves(queries, zh, 1)
    query_other = shifted(query_sent, "zh", 1)

    left = shifted(own, "x", 1)
    right = shifted(own, "x", 3)
    opposite = shifted(left[:4], "x", 1)
    opposed = shifted(right[4:], "x", 3)

    queries_t, *state = suffix_attention(coords, lengths, query_mine, query_other, near, far)
    where = (coords, lengths, hits)

    def both(chunk, back, first):
        return [(chunk, (back, False, first)), (shifted(chunk, "core", 1), (back, True, first))]

    state = prefix_attention(where, queries_t, state, both(own, 0, 0))
    state = prefix_attention(where, queries_t, state, both(left, 1, 0) + both(right, 3, 0))
    chunks = both(opposite, 2, 0) + both(opposed, 2, 4)
    done = prefix_attention(where, queries_t, state, chunks, last=True)[0]
    theirs = shifted(done[1], "zh", 1)
    first = jnp.where(zh == 0, done[0], theirs)
    second = jnp.where(zh == 0, theirs, done[0])
    attended = jnp.concatenate([first, second], axis=1)

    written, left = lax.optimization_barrier((suffix_kv, left))
    layout = written.reshape(2, 4, part_rows, suffix_kv.shape[2])
    layout = lax.all_to_all(layout, "tp", split_axis=1, concat_axis=1, tiled=True)
    incoming = jnp.transpose(layout, (0, 2, 1, 3)).reshape(2, part_rows, pool.shape[3])
    incoming = shifted(incoming, "inst", 1)
    new_pool = write_block(write_slot, pool, incoming)
    return attended, new_pool


def solution(mesh):
    split = Mesh(mesh.devices.reshape(4, 2, 4, 2, 4), ("inst", "zh", "x", "core", "tp"))
    ctx = ("inst", "zh", "x", "core")
    placed = (
        P(ctx, "tp"),
        P(None, ctx, "tp"),
        P(ctx, None, "tp", None),
        P(),
        P(),
        P(ctx, None),
    )
    return jax.shard_map(
        local,
        mesh=split,
        in_specs=placed,
        out_specs=(P(ctx, "tp"), P(ctx, None, "tp", None)),
        check_vma=False,
    )
```

```python
import functools
import math

import jax
import jax.numpy as jnp
from jax import lax
from jax.experimental import pallas as pl
from jax.experimental.pallas import tpu as pltpu
from jax.sharding import Mesh, PartitionSpec as P

HD = 128
BLOCK = 128
NEG = -1e30
SCALE = HD ** -0.5 * math.log2(math.e)
VMEM_LIMIT = 48 * 1024 * 1024
SMEM = pl.BlockSpec(memory_space=pltpu.SMEM)
VMEM = pl.BlockSpec(memory_space=pltpu.VMEM)


def shifted(block, axis, distance):
    count = lax.axis_size(axis)
    return lax.ppermute(block, axis, [(i, (i + distance) % count) for i in range(count)])


def pick_kernel(coords_ref, hits_ref, pool_ref, out_ref, blocks_ref, sems):
    insts, zh, x, core = hits_ref.shape[0], coords_ref[1], coords_ref[2], coords_ref[3]
    owner = ((coords_ref[0] * 2 + zh) * 4 + x) * 2 + core
    copies = []
    for inst in range(insts):
        block = hits_ref[inst, 0, owner]
        for req in range(1, hits_ref.shape[1]):
            block = jnp.maximum(block, hits_ref[inst, req, owner])
        slot = block - owner * pool_ref.shape[0]
        copies.append(
            pltpu.make_async_copy(pool_ref.at[slot], blocks_ref.at[inst], sems.at[inst])
        )
    for copy in copies:
        copy.start()
    for inst, copy in enumerate(copies):
        copy.wait()
        for part in range(8):
            out_ref[inst, part % 2, part // 2] = blocks_ref[
                inst, :, :, part * HD : (part + 1) * HD
            ]


def pick_blocks(coords, hits, pool):
    insts = hits.shape[0]
    _, two, rows, cols = pool.shape
    return pl.pallas_call(
        pick_kernel,
        in_specs=[SMEM, SMEM, pl.BlockSpec(memory_space=pl.ANY)],
        out_specs=VMEM,
        out_shape=jax.ShapeDtypeStruct((insts, 2, 4, two, rows, HD), pool.dtype),
        scratch_shapes=[
            pltpu.VMEM((insts, two, rows, cols), pool.dtype),
            pltpu.SemaphoreType.DMA((insts,)),
        ],
        name="pick_blocks",
    )(coords, hits, pool)


def step(unit, keys, values, queries_ref, high_ref, total_ref, acc_ref):
    scores = SCALE * jnp.dot(keys, queries_ref[unit], preferred_element_type=jnp.float32)
    before = high_ref[unit]
    high = jnp.maximum(before, jnp.max(scores, axis=0, keepdims=True))
    faded = jnp.exp2(before - high)
    weights = jnp.exp2(scores - high)
    high_ref[unit] = high
    total_ref[unit] = total_ref[unit] * faded + jnp.sum(weights, axis=0, keepdims=True)
    summed = jnp.dot(values, weights.astype(jnp.bfloat16), preferred_element_type=jnp.float32)
    acc_ref[unit] = acc_ref[unit] * faded + summed


def first_step(unit, keys, values, queries_ref, high_ref, total_ref, acc_ref):
    scores = SCALE * jnp.dot(keys, queries_ref[unit], preferred_element_type=jnp.float32)
    key_at = lax.broadcasted_iota(jnp.int32, scores.shape, 0)
    query_at = lax.rem(lax.broadcasted_iota(jnp.int32, scores.shape, 1), BLOCK)
    scores = jnp.where(key_at <= query_at, scores, NEG)
    high = jnp.max(scores, axis=0, keepdims=True)
    weights = jnp.exp2(scores - high)
    high_ref[unit] = high
    total_ref[unit] = jnp.sum(weights, axis=0, keepdims=True)
    acc_ref[unit] = jnp.dot(
        values.T, weights.astype(jnp.bfloat16), preferred_element_type=jnp.float32
    )


def sweep(units, wanted_of, loads, keys_ref, values_ref, state):
    for held, unit in enumerate(units):
        count = jnp.int32(0)
        for place, load in enumerate(loads):
            wanted = wanted_of(unit, place)

            @pl.when(wanted)
            def _(count=count, load=load):
                keys, values = load()
                span = pl.ds(pl.multiple_of(count * BLOCK, BLOCK), BLOCK)
                keys_ref[span, :] = keys
                values_ref[span, :] = values

            count = count + wanted.astype(jnp.int32)

        def many(first, blocks, held=held):
            span = pl.ds(pl.multiple_of(first * BLOCK, BLOCK), blocks * BLOCK)
            step(held, keys_ref[span, :], values_ref[span, :].T, *state)

        def turn(index, carry, many=many):
            many(index * 4, 4)
            return carry

        lax.fori_loop(0, count // 4, turn, 0)
        for rest in (1, 2, 3):

            @pl.when(count % 4 == rest)
            def _(count=count, many=many, rest=rest):
                many(count // 4 * 4, rest)


def unit_places(coords_ref):
    zh, x, core = coords_ref[1], coords_ref[2], coords_ref[3]
    return (zh * 4 + x) * 2 + core, ((1 - zh) * 4 + x) * 2 + core


def request_at(lengths_ref, inst, place):
    first = lengths_ref[inst, 0]
    second = first + lengths_ref[inst, 1]
    third = second + lengths_ref[inst, 2]
    return sum((place >= edge).astype(jnp.int32) for edge in (first, second, third))


def suffix_kernel(coords_ref, lengths_ref, mine_ref, other_ref, near_ref, far_ref, *refs):
    queries_ref, high_ref, total_ref, acc_ref, keys_ref, values_ref = refs
    state = (queries_ref, high_ref, total_ref, acc_ref)
    for unit, source in enumerate((mine_ref, other_ref)):
        for head in range(queries_ref.shape[2] // HD):
            cols = slice(head * HD, (head + 1) * HD)
            queries_ref[unit, :, cols] = source[:, cols].T
        first_step(unit, near_ref[0, unit, :, :HD], near_ref[0, unit, :, HD:], *state)
    inst, zh, x, core = (coords_ref[i] for i in range(4))
    units = unit_places(coords_ref)
    unit_reqs = [request_at(lengths_ref, inst, place) for place in units]
    loads, places = [], []
    for turned, source in enumerate((near_ref, far_ref)):
        for back in range(4):
            for side in range(2):
                loads.append(lambda s=source, b=back, h=side: (s[b, h, :, :HD], s[b, h, :, HD:]))
                from_zh = 1 - zh if side else zh
                from_core = 1 - core if turned else core
                places.append((from_zh * 4 + lax.rem(x - back + 4, 4)) * 2 + from_core)
    reqs = [request_at(lengths_ref, inst, place) for place in places]

    def wanted_of(unit, index):
        return (places[index] < units[unit]) & (reqs[index] == unit_reqs[unit])

    sweep((0, 1), wanted_of, loads, keys_ref, values_ref, state)


def prefix_kernel(origins, chosen, last, coords_ref, lengths_ref, hits_ref, queries_ref, *refs):
    high_in, total_in, acc_in, refs = refs[0], refs[1], refs[2], refs[3:]
    chunks, refs = refs[: len(origins)], refs[len(origins) :]
    if last:
        out_ref, high_ref, total_ref, acc_ref, keys_ref, values_ref = refs
    else:
        high_ref, total_ref, acc_ref, keys_ref, values_ref = refs
    high_ref[...] = high_in[...]
    total_ref[...] = total_in[...]
    acc_ref[...] = acc_in[...]
    state = (queries_ref, high_ref, total_ref, acc_ref)
    inst, _, x, core = (coords_ref[i] for i in range(4))
    reqs = [request_at(lengths_ref, inst, place) for place in unit_places(coords_ref)]
    loads, owners = [], []
    for chunk, (back, turned, first) in zip(chunks, origins):
        from_x = lax.rem(x - back + 4, 4)
        from_core = 1 - core if turned else core
        for place in range(chunk.shape[0]):

            def load(chunk=chunk, place=place):
                shape = (BLOCK, HD)
                return chunk[place, :, 0].reshape(shape), chunk[place, :, 1].reshape(shape)

            loads.append(load)
            owners.append((first + place) * 8 + from_x * 2 + from_core)

    def wanted_of(unit, index):
        return hits_ref[inst, reqs[unit], owners[index]] >= 0

    sweep(chosen, wanted_of, loads, keys_ref, values_ref, state)
    if last:
        for held in range(len(chosen)):
            for head in range(out_ref.shape[1] // HD):
                cols = slice(head * HD, (head + 1) * HD)
                done = acc_ref[held, :, cols] / total_ref[held, :, cols]
                out_ref[:, cols] = done.T.astype(out_ref.dtype)


def write_kernel(coords_ref, slot_ref, pool_ref, *refs):
    pieces, out_ref = refs[:-1], refs[-1]
    out_ref[...] = pool_ref[...]
    held = pool_ref.shape[0]
    slot = slot_ref[0, 0]

    @pl.when(slot // held == pl.program_id(0))
    def _():
        for back, piece in enumerate(pieces):
            width = piece.shape[2]
            source = lax.rem(coords_ref[4] - back + 4, 4)
            cols = pl.ds(pl.multiple_of(source * width, width), width)
            out_ref[lax.rem(slot, held), :, :, cols] = piece[...]


def write_block(coords, slots, pool, pieces):
    count = pool.shape[0]
    steps = 4
    blocked = pl.BlockSpec((count // steps,) + pool.shape[1:], lambda i: (i, 0, 0, 0))
    return pl.pallas_call(
        write_kernel,
        grid=(steps,),
        in_specs=[SMEM, SMEM, blocked] + [VMEM] * len(pieces),
        out_specs=blocked,
        out_shape=jax.ShapeDtypeStruct(pool.shape, pool.dtype),
        cost_estimate=pl.CostEstimate(flops=0, bytes_accessed=4 * pool.size, transcendentals=0),
        name="write_block",
    )(coords, slots, pool, *pieces)


def scratch(block_count):
    return [
        pltpu.VMEM((block_count * BLOCK, HD), jnp.bfloat16),
        pltpu.VMEM((block_count * BLOCK, HD), jnp.bfloat16),
    ]


def cost(block_count, rows):
    flops = 4 * block_count * BLOCK * HD * rows
    return pl.CostEstimate(flops=flops, bytes_accessed=4 << 20, transcendentals=0)


def state_shapes(rows):
    return [
        jax.ShapeDtypeStruct((2, 1, rows), jnp.float32),
        jax.ShapeDtypeStruct((2, 1, rows), jnp.float32),
        jax.ShapeDtypeStruct((2, HD, rows), jnp.float32),
    ]


def suffix_attention(coords, lengths, mine, other, near, far):
    rows = mine.shape[1]
    return pl.pallas_call(
        suffix_kernel,
        in_specs=[SMEM] * 2 + [VMEM] * 4,
        out_specs=[VMEM] * 4,
        out_shape=[jax.ShapeDtypeStruct((2, HD, rows), jnp.bfloat16)] + state_shapes(rows),
        scratch_shapes=scratch(16),
        compiler_params=pltpu.CompilerParams(vmem_limit_bytes=VMEM_LIMIT),
        cost_estimate=cost(8, 2 * rows),
        name="suffix_attention",
    )(coords, lengths, mine, other, near, far)


def prefix_attention(where, queries_t, state, chunks, last_of=None):
    rows = queries_t.shape[2]
    arrays = [chunk for chunk, _ in chunks]
    block_count = sum(array.shape[0] for array in arrays)
    last = last_of is not None
    chosen = (last_of,) if last else (0, 1)
    if last:
        held = [
            pl.BlockSpec((1,) + array.shape[1:], lambda i: (last_of, 0, 0))
            for array in (queries_t, *state)
        ]
        out_shape = [jax.ShapeDtypeStruct((BLOCK, rows), jnp.bfloat16)]
        extra = [pltpu.VMEM((1,) + shape.shape[1:], shape.dtype) for shape in state_shapes(rows)]
    else:
        held = [VMEM] * 4
        out_shape, extra = state_shapes(rows), []
    return pl.pallas_call(
        functools.partial(prefix_kernel, [origin for _, origin in chunks], chosen, last),
        grid=(1,),
        in_specs=[SMEM] * 3 + held + [VMEM] * len(arrays),
        out_specs=[VMEM] * len(out_shape),
        out_shape=out_shape,
        scratch_shapes=extra + scratch(block_count),
        compiler_params=pltpu.CompilerParams(vmem_limit_bytes=VMEM_LIMIT),
        cost_estimate=cost(block_count, len(chosen) * rows),
        name="prefix_attention",
    )(*where, queries_t, *state, *arrays)


def halves(array, side, axis):
    first, second = jnp.split(array, 2, axis=axis)
    return jnp.where(side == 0, first, second), jnp.where(side == 0, second, first)


def local(queries, suffix_kv, pool, hits, lengths, write_slot):
    names = ("inst", "zh", "x", "core", "tp")
    coords = jnp.stack([lax.axis_index(name) for name in names]).astype(jnp.int32)
    zh = lax.axis_index("zh")
    part_rows = pool.shape[2]

    query_mine, query_sent = halves(queries, zh, 1)
    suffix_mine, suffix_sent = halves(suffix_kv, zh, 2)
    joined = jnp.concatenate([query_sent, suffix_sent[0], suffix_sent[1]], axis=1)
    joined = shifted(joined, "zh", 1)

    sent = pick_blocks(coords, hits, pool).reshape(32, 2, part_rows, HD)
    fetched = lax.all_to_all(sent, ("inst", "zh", "tp"), split_axis=0, concat_axis=0, tiled=True)
    own = fetched.reshape(8, 4, 2, part_rows, HD)

    suffix_mine = jnp.concatenate([suffix_mine[0], suffix_mine[1]], axis=1)
    near = jnp.stack([suffix_mine, joined[:, query_mine.shape[1] :]])
    near = jnp.stack([near] + [shifted(near, "x", far) for far in (1, 2, 3)])
    far = shifted(near, "core", 1)
    queries_t, *state = suffix_attention(coords, lengths, query_mine, joined, near, far)

    left = shifted(own, "x", 1)
    right = shifted(own, "x", 3)
    opposite = shifted(left[:4], "x", 1)
    opposed = shifted(right[4:], "x", 3)
    where = (coords, lengths, hits)

    def both(chunk, back, first):
        return [(chunk, (back, False, first)), (shifted(chunk, "core", 1), (back, True, first))]

    state = prefix_attention(where, queries_t, state, both(own, 0, 0))
    state = prefix_attention(where, queries_t, state, both(left, 1, 0) + both(right, 3, 0))
    chunks = both(opposite, 2, 0) + both(opposed, 2, 4)
    for_other = prefix_attention(where, queries_t, state, chunks, last_of=1)[0]
    theirs = shifted(for_other, "zh", 1)
    mine = prefix_attention(where, queries_t, state, chunks, last_of=0)[0]
    first = jnp.where(zh == 0, mine, theirs)
    second = jnp.where(zh == 0, theirs, mine)
    attended = jnp.concatenate([first, second], axis=1)

    written, _ = lax.optimization_barrier((suffix_kv, joined))
    written = shifted(written, "inst", 1)
    written, _ = lax.optimization_barrier((written, left))
    turned = lax.dynamic_slice_in_dim(
        jnp.concatenate([written, written], axis=1),
        lax.axis_index("tp") * part_rows,
        written.shape[1],
        axis=1,
    )
    pieces = [turned[:, back * part_rows : (back + 1) * part_rows] for back in range(4)]
    pieces = [shifted(piece, "tp", back) if back else piece for back, piece in enumerate(pieces)]
    pieces, _ = lax.optimization_barrier((pieces, mine))
    new_pool = write_block(coords, write_slot, pool, pieces)
    return attended, new_pool


def solution(mesh):
    split = Mesh(mesh.devices.reshape(4, 2, 4, 2, 4), ("inst", "zh", "x", "core", "tp"))
    ctx = ("inst", "zh", "x", "core")
    placed = (
        P(ctx, "tp"),
        P(None, ctx, "tp"),
        P(ctx, None, "tp", None),
        P(),
        P(),
        P(ctx, None),
    )
    return jax.shard_map(
        local,
        mesh=split,
        in_specs=placed,
        out_specs=(P(ctx, "tp"), P(ctx, None, "tp", None)),
        check_vma=False,
    )
```

```python
import functools
import math

import jax
import jax.numpy as jnp
from jax import lax
from jax.experimental import pallas as pl
from jax.experimental.pallas import tpu as pltpu
from jax.sharding import Mesh, PartitionSpec as P

HD = 128
BLOCK = 128
NEG = -1e30
MARGIN = 64.0
SCALE = HD ** -0.5 * math.log2(math.e)
VMEM_LIMIT = 48 * 1024 * 1024
SMEM = pl.BlockSpec(memory_space=pltpu.SMEM)
VMEM = pl.BlockSpec(memory_space=pltpu.VMEM)


def shifted(block, axis, distance):
    count = lax.axis_size(axis)
    return lax.ppermute(block, axis, [(i, (i + distance) % count) for i in range(count)])


def pick_kernel(coords_ref, hits_ref, pool_ref, out_ref, blocks_ref, sems):
    insts, zh, x, core = hits_ref.shape[0], coords_ref[1], coords_ref[2], coords_ref[3]
    owner = ((coords_ref[0] * 2 + zh) * 4 + x) * 2 + core
    copies = []
    for inst in range(insts):
        block = hits_ref[inst, 0, owner]
        for req in range(1, hits_ref.shape[1]):
            block = jnp.maximum(block, hits_ref[inst, req, owner])
        slot = block - owner * pool_ref.shape[0]
        copies.append(
            pltpu.make_async_copy(pool_ref.at[slot], blocks_ref.at[inst], sems.at[inst])
        )
    for copy in copies:
        copy.start()
    for inst, copy in enumerate(copies):
        copy.wait()
        for part in range(8):
            out_ref[inst, part % 2, part // 2] = blocks_ref[
                inst, :, :, part * HD : (part + 1) * HD
            ]


def pick_blocks(coords, hits, pool):
    insts = hits.shape[0]
    _, two, rows, cols = pool.shape
    return pl.pallas_call(
        pick_kernel,
        in_specs=[SMEM, SMEM, pl.BlockSpec(memory_space=pl.ANY)],
        out_specs=VMEM,
        out_shape=jax.ShapeDtypeStruct((insts, 2, 4, two, rows, HD), pool.dtype),
        scratch_shapes=[
            pltpu.VMEM((insts, two, rows, cols), pool.dtype),
            pltpu.SemaphoreType.DMA((insts,)),
        ],
        name="pick_blocks",
    )(coords, hits, pool)


def step(unit, keys, values, queries_ref, high_ref, total_ref, acc_ref):
    scores = SCALE * jnp.dot(keys, queries_ref[unit], preferred_element_type=jnp.float32)
    before = high_ref[unit]
    high = jnp.maximum(before, jnp.max(scores, axis=0, keepdims=True))
    faded = jnp.exp2(before - high)
    weights = jnp.exp2(scores - high)
    high_ref[unit] = high
    total_ref[unit] = total_ref[unit] * faded + jnp.sum(weights, axis=0, keepdims=True)
    summed = jnp.dot(values, weights.astype(jnp.bfloat16), preferred_element_type=jnp.float32)
    acc_ref[unit] = acc_ref[unit] * faded + summed


def quick_step(unit, keys, values, queries_ref, high_ref, total_ref, acc_ref, top_ref):
    scores = SCALE * jnp.dot(keys, queries_ref[unit], preferred_element_type=jnp.float32)
    top_ref[...] = jnp.maximum(top_ref[...], jnp.max(scores, axis=0, keepdims=True))
    weights = jnp.exp2(scores - high_ref[unit])
    total_ref[unit] += jnp.sum(weights, axis=0, keepdims=True)
    acc_ref[unit] += jnp.dot(
        values, weights.astype(jnp.bfloat16), preferred_element_type=jnp.float32
    )


def first_step(unit, keys, values, queries_ref, high_ref, total_ref, acc_ref):
    scores = SCALE * jnp.dot(keys, queries_ref[unit], preferred_element_type=jnp.float32)
    key_at = lax.broadcasted_iota(jnp.int32, scores.shape, 0)
    query_at = lax.rem(lax.broadcasted_iota(jnp.int32, scores.shape, 1), BLOCK)
    scores = jnp.where(key_at <= query_at, scores, NEG)
    high = jnp.max(scores, axis=0, keepdims=True)
    weights = jnp.exp2(scores - high)
    high_ref[unit] = high
    total_ref[unit] = jnp.sum(weights, axis=0, keepdims=True)
    acc_ref[unit] = jnp.dot(
        values.T, weights.astype(jnp.bfloat16), preferred_element_type=jnp.float32
    )


def gather(unit, wanted_of, loads, keys_ref, values_ref):
    count = jnp.int32(0)
    for place, load in enumerate(loads):
        wanted = wanted_of(unit, place)

        @pl.when(wanted)
        def _(count=count, load=load):
            keys, values = load()
            span = pl.ds(pl.multiple_of(count * BLOCK, BLOCK), BLOCK)
            keys_ref[span, :] = keys
            values_ref[span, :] = values

        count = count + wanted.astype(jnp.int32)
    return count


def sweep(held, count, widths, keys_ref, values_ref, one_step, state):
    def many(first, blocks):
        span = pl.ds(pl.multiple_of(first * BLOCK, BLOCK), blocks * BLOCK)
        one_step(held, keys_ref[span, :], values_ref[span, :].T, *state)

    widest = widths[0]

    def turn(index, carry):
        many(index * widest, widest)
        return carry

    lax.fori_loop(0, count // widest, turn, 0)
    done = count // widest * widest
    for width in widths[1:]:
        fits = count - done >= width
        pl.when(fits)(functools.partial(many, done, width))
        done = done + jnp.where(fits, width, 0)


def unit_places(coords_ref):
    zh, x, core = coords_ref[1], coords_ref[2], coords_ref[3]
    return (zh * 4 + x) * 2 + core, ((1 - zh) * 4 + x) * 2 + core


def request_at(lengths_ref, inst, place):
    first = lengths_ref[inst, 0]
    second = first + lengths_ref[inst, 1]
    third = second + lengths_ref[inst, 2]
    return sum((place >= edge).astype(jnp.int32) for edge in (first, second, third))


def suffix_kernel(coords_ref, lengths_ref, mine_ref, other_ref, near_ref, far_ref, *refs):
    queries_ref, high_ref, total_ref, acc_ref, keys_ref, values_ref = refs
    state = (queries_ref, high_ref, total_ref, acc_ref)
    for unit, source in enumerate((mine_ref, other_ref)):
        for head in range(queries_ref.shape[2] // HD):
            cols = slice(head * HD, (head + 1) * HD)
            queries_ref[unit, :, cols] = source[:, cols].T
        first_step(unit, near_ref[0, unit, :, :HD], near_ref[0, unit, :, HD:], *state)
    inst, zh, x, core = (coords_ref[i] for i in range(4))
    units = unit_places(coords_ref)
    unit_reqs = [request_at(lengths_ref, inst, place) for place in units]
    loads, places = [], []
    for turned, source in enumerate((near_ref, far_ref)):
        for back in range(4):
            for side in range(2):
                loads.append(lambda s=source, b=back, h=side: (s[b, h, :, :HD], s[b, h, :, HD:]))
                from_zh = 1 - zh if side else zh
                from_core = 1 - core if turned else core
                places.append((from_zh * 4 + lax.rem(x - back + 4, 4)) * 2 + from_core)
    reqs = [request_at(lengths_ref, inst, place) for place in places]

    def wanted_of(unit, index):
        return (places[index] < units[unit]) & (reqs[index] == unit_reqs[unit])

    for unit in range(2):
        count = gather(unit, wanted_of, loads, keys_ref, values_ref)
        sweep(unit, count, (2, 1), keys_ref, values_ref, step, state)


def prefix_kernel(origins, chosen, last, coords_ref, lengths_ref, hits_ref, queries_ref, *refs):
    high_in, total_in, acc_in, refs = refs[0], refs[1], refs[2], refs[3:]
    chunks, refs = refs[: len(origins)], refs[len(origins) :]
    out_ref, refs = (refs[0], refs[1:]) if last else (None, refs)
    high_ref, total_ref, acc_ref, keys_ref, values_ref, top_ref = refs
    state = (queries_ref, high_ref, total_ref, acc_ref)
    inst, _, x, core = (coords_ref[i] for i in range(4))
    reqs = [request_at(lengths_ref, inst, place) for place in unit_places(coords_ref)]
    loads, owners = [], []
    for chunk, (back, turned, first) in zip(chunks, origins):
        from_x = lax.rem(x - back + 4, 4)
        from_core = 1 - core if turned else core
        for place in range(chunk.shape[0]):

            def load(chunk=chunk, place=place):
                shape = (BLOCK, HD)
                return chunk[place, :, 0].reshape(shape), chunk[place, :, 1].reshape(shape)

            loads.append(load)
            owners.append((first + place) * 8 + from_x * 2 + from_core)

    def wanted_of(unit, index):
        return hits_ref[inst, reqs[unit], owners[index]] >= 0

    for held, unit in enumerate(chosen):

        def begin(held=held):
            high_ref[held] = high_in[held]
            total_ref[held] = total_in[held]
            acc_ref[held] = acc_in[held]

        begin()
        top_ref[...] = high_in[held]
        count = gather(unit, wanted_of, loads, keys_ref, values_ref)
        quick = state + (top_ref,)
        sweep(held, count, (8, 4, 2, 1), keys_ref, values_ref, quick_step, quick)
        above = jnp.max(top_ref[...] - high_in[held])

        @pl.when(above > MARGIN)
        def _(held=held, count=count, begin=begin):
            begin()
            sweep(held, count, (2, 1), keys_ref, values_ref, step, state)

    if last:
        for held in range(len(chosen)):
            for head in range(out_ref.shape[1] // HD):
                cols = slice(head * HD, (head + 1) * HD)
                done = acc_ref[held, :, cols] / total_ref[held, :, cols]
                out_ref[:, cols] = done.T.astype(out_ref.dtype)


def write_kernel(coords_ref, slot_ref, pool_ref, *refs):
    pieces, out_ref = refs[:-1], refs[-1]
    out_ref[...] = pool_ref[...]
    held = pool_ref.shape[0]
    slot = slot_ref[0, 0]

    @pl.when(slot // held == pl.program_id(0))
    def _():
        for back, piece in enumerate(pieces):
            width = piece.shape[2]
            source = lax.rem(coords_ref[4] - back + 4, 4)
            cols = pl.ds(pl.multiple_of(source * width, width), width)
            out_ref[lax.rem(slot, held), :, :, cols] = piece[...]


def write_block(coords, slots, pool, pieces):
    count = pool.shape[0]
    steps = 4
    blocked = pl.BlockSpec((count // steps,) + pool.shape[1:], lambda i: (i, 0, 0, 0))
    return pl.pallas_call(
        write_kernel,
        grid=(steps,),
        in_specs=[SMEM, SMEM, blocked] + [VMEM] * len(pieces),
        out_specs=blocked,
        out_shape=jax.ShapeDtypeStruct(pool.shape, pool.dtype),
        cost_estimate=pl.CostEstimate(flops=0, bytes_accessed=4 * pool.size, transcendentals=0),
        name="write_block",
    )(coords, slots, pool, *pieces)


def scratch(block_count):
    return [
        pltpu.VMEM((block_count * BLOCK, HD), jnp.bfloat16),
        pltpu.VMEM((block_count * BLOCK, HD), jnp.bfloat16),
    ]


def cost(block_count, rows):
    flops = 4 * block_count * BLOCK * HD * rows
    return pl.CostEstimate(flops=flops, bytes_accessed=4 << 20, transcendentals=0)


def state_shapes(rows):
    return [
        jax.ShapeDtypeStruct((2, 1, rows), jnp.float32),
        jax.ShapeDtypeStruct((2, 1, rows), jnp.float32),
        jax.ShapeDtypeStruct((2, HD, rows), jnp.float32),
    ]


def suffix_attention(coords, lengths, mine, other, near, far):
    rows = mine.shape[1]
    return pl.pallas_call(
        suffix_kernel,
        in_specs=[SMEM] * 2 + [VMEM] * 4,
        out_specs=[VMEM] * 4,
        out_shape=[jax.ShapeDtypeStruct((2, HD, rows), jnp.bfloat16)] + state_shapes(rows),
        scratch_shapes=scratch(16),
        compiler_params=pltpu.CompilerParams(vmem_limit_bytes=VMEM_LIMIT),
        cost_estimate=cost(8, 2 * rows),
        name="suffix_attention",
    )(coords, lengths, mine, other, near, far)


def prefix_attention(where, queries_t, state, chunks, last_of=None):
    rows = queries_t.shape[2]
    arrays = [chunk for chunk, _ in chunks]
    block_count = sum(array.shape[0] for array in arrays)
    last = last_of is not None
    chosen = (last_of,) if last else (0, 1)
    if last:
        held = [
            pl.BlockSpec((1,) + array.shape[1:], lambda i: (last_of, 0, 0))
            for array in (queries_t, *state)
        ]
        out_shape = [jax.ShapeDtypeStruct((BLOCK, rows), jnp.bfloat16)]
        extra = [pltpu.VMEM((1,) + shape.shape[1:], shape.dtype) for shape in state_shapes(rows)]
    else:
        held = [VMEM] * 4
        out_shape, extra = state_shapes(rows), []
    return pl.pallas_call(
        functools.partial(prefix_kernel, [origin for _, origin in chunks], chosen, last),
        grid=(1,),
        in_specs=[SMEM] * 3 + held + [VMEM] * len(arrays),
        out_specs=[VMEM] * len(out_shape),
        out_shape=out_shape,
        scratch_shapes=extra + scratch(block_count) + [pltpu.VMEM((1, rows), jnp.float32)],
        compiler_params=pltpu.CompilerParams(vmem_limit_bytes=VMEM_LIMIT),
        cost_estimate=cost(block_count, len(chosen) * rows),
        name="prefix_attention",
    )(*where, queries_t, *state, *arrays)


def halves(array, side, axis):
    first, second = jnp.split(array, 2, axis=axis)
    return jnp.where(side == 0, first, second), jnp.where(side == 0, second, first)


def local(queries, suffix_kv, pool, hits, lengths, write_slot):
    names = ("inst", "zh", "x", "core", "tp")
    coords = jnp.stack([lax.axis_index(name) for name in names]).astype(jnp.int32)
    zh = lax.axis_index("zh")
    part_rows = pool.shape[2]

    query_mine, query_sent = halves(queries, zh, 1)
    suffix_mine, suffix_sent = halves(suffix_kv, zh, 2)
    joined = jnp.concatenate([query_sent, suffix_sent[0], suffix_sent[1]], axis=1)
    joined = shifted(joined, "zh", 1)

    sent = pick_blocks(coords, hits, pool).reshape(32, 2, part_rows, HD)
    sent, joined = lax.optimization_barrier((sent, joined))
    fetched = lax.all_to_all(sent, ("inst", "zh", "tp"), split_axis=0, concat_axis=0, tiled=True)
    own = fetched.reshape(8, 4, 2, part_rows, HD)

    suffix_mine = jnp.concatenate([suffix_mine[0], suffix_mine[1]], axis=1)
    near = jnp.stack([suffix_mine, joined[:, query_mine.shape[1] :]])
    near = jnp.stack([near] + [shifted(near, "x", far) for far in (1, 2, 3)])
    far = shifted(near, "core", 1)
    queries_t, *state = suffix_attention(coords, lengths, query_mine, joined, near, far)

    left = shifted(own, "x", 1)
    right = shifted(own, "x", 3)
    opposite = shifted(left[:4], "x", 1)
    opposed = shifted(right[4:], "x", 3)
    where = (coords, lengths, hits)

    def both(chunk, back, first):
        return [(chunk, (back, False, first)), (shifted(chunk, "core", 1), (back, True, first))]

    state = prefix_attention(where, queries_t, state, both(own, 0, 0))
    state = prefix_attention(where, queries_t, state, both(left, 1, 0) + both(right, 3, 0))
    chunks = both(opposite, 2, 0) + both(opposed, 2, 4)
    for_other = prefix_attention(where, queries_t, state, chunks, last_of=1)[0]
    theirs = shifted(for_other, "zh", 1)
    mine = prefix_attention(where, queries_t, state, chunks, last_of=0)[0]
    first = jnp.where(zh == 0, mine, theirs)
    second = jnp.where(zh == 0, theirs, mine)
    attended = jnp.concatenate([first, second], axis=1)

    written, _ = lax.optimization_barrier((suffix_kv, joined))
    written = shifted(written, "inst", 1)
    written, _ = lax.optimization_barrier((written, left))
    turned = lax.dynamic_slice_in_dim(
        jnp.concatenate([written, written], axis=1),
        lax.axis_index("tp") * part_rows,
        written.shape[1],
        axis=1,
    )
    pieces = [turned[:, back * part_rows : (back + 1) * part_rows] for back in range(4)]
    pieces = [shifted(piece, "tp", back) if back else piece for back, piece in enumerate(pieces)]
    pieces, _ = lax.optimization_barrier((pieces, mine))
    new_pool = write_block(coords, write_slot, pool, pieces)
    return attended, new_pool


def solution(mesh):
    split = Mesh(mesh.devices.reshape(4, 2, 4, 2, 4), ("inst", "zh", "x", "core", "tp"))
    ctx = ("inst", "zh", "x", "core")
    placed = (
        P(ctx, "tp"),
        P(None, ctx, "tp"),
        P(ctx, None, "tp", None),
        P(),
        P(),
        P(ctx, None),
    )
    return jax.shard_map(
        local,
        mesh=split,
        in_specs=placed,
        out_specs=(P(ctx, "tp"), P(ctx, None, "tp", None)),
        check_vma=False,
    )
```

```python
import functools
import math

import jax
import jax.numpy as jnp
from jax import lax
from jax.experimental import pallas as pl
from jax.experimental.pallas import tpu as pltpu
from jax.sharding import Mesh, PartitionSpec as P

HD = 128
BLOCK = 128
NEG = -1e30
MARGIN = 64.0
SCALE = HD ** -0.5 * math.log2(math.e)
VMEM_LIMIT = 48 * 1024 * 1024
SMEM = pl.BlockSpec(memory_space=pltpu.SMEM)
VMEM = pl.BlockSpec(memory_space=pltpu.VMEM)


def shifted(block, axis, distance):
    count = lax.axis_size(axis)
    return lax.ppermute(block, axis, [(i, (i + distance) % count) for i in range(count)])


def pick_kernel(coords_ref, hits_ref, pool_ref, out_ref, blocks_ref, sems):
    insts, zh, x, core = hits_ref.shape[0], coords_ref[1], coords_ref[2], coords_ref[3]
    owner = ((coords_ref[0] * 2 + zh) * 4 + x) * 2 + core
    copies = []
    for inst in range(insts):
        block = hits_ref[inst, 0, owner]
        for req in range(1, hits_ref.shape[1]):
            block = jnp.maximum(block, hits_ref[inst, req, owner])
        slot = block - owner * pool_ref.shape[0]
        copies.append(
            pltpu.make_async_copy(pool_ref.at[slot], blocks_ref.at[inst], sems.at[inst])
        )
    for copy in copies:
        copy.start()
    for inst, copy in enumerate(copies):
        copy.wait()
        for part in range(8):
            out_ref[inst, part % 2, part // 2] = blocks_ref[
                inst, :, :, part * HD : (part + 1) * HD
            ]


def pick_blocks(coords, hits, pool):
    insts = hits.shape[0]
    _, two, rows, cols = pool.shape
    return pl.pallas_call(
        pick_kernel,
        in_specs=[SMEM, SMEM, pl.BlockSpec(memory_space=pl.ANY)],
        out_specs=VMEM,
        out_shape=jax.ShapeDtypeStruct((insts, 2, 4, two, rows, HD), pool.dtype),
        scratch_shapes=[
            pltpu.VMEM((insts, two, rows, cols), pool.dtype),
            pltpu.SemaphoreType.DMA((insts,)),
        ],
        name="pick_blocks",
    )(coords, hits, pool)


def scored(keys, queries_ref):
    return SCALE * jnp.dot(keys, queries_ref[...], preferred_element_type=jnp.float32)


def weighed(values, weights):
    return jnp.dot(values.T, weights.astype(jnp.bfloat16), preferred_element_type=jnp.float32)


def first_step(keys, values, queries_ref, high_ref, total_ref, acc_ref):
    scores = scored(keys, queries_ref)
    key_at = lax.broadcasted_iota(jnp.int32, scores.shape, 0)
    query_at = lax.rem(lax.broadcasted_iota(jnp.int32, scores.shape, 1), BLOCK)
    scores = jnp.where(key_at <= query_at, scores, NEG)
    high = jnp.max(scores, axis=0, keepdims=True)
    weights = jnp.exp2(scores - high)
    high_ref[...] = high
    total_ref[...] = jnp.sum(weights, axis=0, keepdims=True)
    acc_ref[...] = weighed(values, weights)


def step(keys, values, queries_ref, high_ref, total_ref, acc_ref):
    scores = scored(keys, queries_ref)
    before = high_ref[...]
    high = jnp.maximum(before, jnp.max(scores, axis=0, keepdims=True))
    faded = jnp.exp2(before - high)
    weights = jnp.exp2(scores - high)
    high_ref[...] = high
    total_ref[...] = total_ref[...] * faded + jnp.sum(weights, axis=0, keepdims=True)
    acc_ref[...] = acc_ref[...] * faded + weighed(values, weights)


def quick_step(keys, values, queries_ref, high_ref, total_ref, acc_ref, top_ref):
    scores = scored(keys, queries_ref)
    top_ref[...] = jnp.maximum(top_ref[...], jnp.max(scores, axis=0, keepdims=True))
    weights = jnp.exp2(scores - high_ref[...])
    total_ref[...] += jnp.sum(weights, axis=0, keepdims=True)
    acc_ref[...] += weighed(values, weights)


def gather(loads, keys_ref, values_ref):
    count = jnp.int32(0)
    for wanted, load in loads:

        @pl.when(wanted)
        def _(count=count, load=load):
            keys, values = load()
            span = pl.ds(pl.multiple_of(count * BLOCK, BLOCK), BLOCK)
            keys_ref[span, :] = keys
            values_ref[span, :] = values

        count = count + wanted.astype(jnp.int32)
    return count


def sweep(count, widths, keys_ref, values_ref, one_step, state):
    def many(first, blocks):
        span = pl.ds(pl.multiple_of(first * BLOCK, BLOCK), blocks * BLOCK)
        one_step(keys_ref[span, :], values_ref[span, :], *state)

    widest = widths[0]

    def turn(index, carry):
        many(index * widest, widest)
        return carry

    lax.fori_loop(0, count // widest, turn, 0)
    done = count // widest * widest
    for width in widths[1:]:
        fits = count - done >= width
        pl.when(fits)(functools.partial(many, done, width))
        done = done + jnp.where(fits, width, 0)


def request_at(lengths_ref, inst, place):
    first = lengths_ref[inst, 0]
    second = first + lengths_ref[inst, 1]
    third = second + lengths_ref[inst, 2]
    return sum((place >= edge).astype(jnp.int32) for edge in (first, second, third))


def attention_kernel(unit, opens, origins, last, coords_ref, lengths_ref, hits_ref, *refs):
    given, refs = refs[: 3 if opens else 4], refs[3 if opens else 4 :]
    chunks, refs = refs[: len(origins)], refs[len(origins) :]
    if opens:
        query_ref, near_ref, far_ref = given
        queries_ref, refs = refs[0], refs[1:]
    else:
        queries_ref, high_in, total_in, acc_in = given
    if last:
        out_ref, refs = refs[0], refs[1:]
    high_ref, total_ref, acc_ref, keys_ref, values_ref, top_ref = refs
    state = (queries_ref, high_ref, total_ref, acc_ref)
    inst, zh, x, core = (coords_ref[i] for i in range(4))
    here = ((1 - zh if unit else zh) * 4 + x) * 2 + core
    req = request_at(lengths_ref, inst, here)
    loads = []

    if opens:
        for head in range(queries_ref.shape[1] // HD):
            cols = slice(head * HD, (head + 1) * HD)
            queries_ref[:, cols] = query_ref[:, cols].T
        for turned, source in enumerate((near_ref, far_ref)):
            for back in range(4):
                for side in range(2):
                    from_zh = 1 - zh if side else zh
                    from_core = 1 - core if turned else core
                    place = (from_zh * 4 + lax.rem(x - back + 4, 4)) * 2 + from_core
                    wanted = (place < here) & (request_at(lengths_ref, inst, place) == req)
                    rows = (lambda s=source, b=back, h=side: (s[b, h, :, :HD], s[b, h, :, HD:]))
                    loads.append((wanted, rows))

        def begin():
            first_step(near_ref[0, unit, :, :HD], near_ref[0, unit, :, HD:], *state)

    else:

        def begin():
            high_ref[...] = high_in[...]
            total_ref[...] = total_in[...]
            acc_ref[...] = acc_in[...]

    for chunk, (back, turned, first) in zip(chunks, origins):
        from_x = lax.rem(x - back + 4, 4)
        from_core = 1 - core if turned else core
        for place in range(chunk.shape[0]):

            def rows(chunk=chunk, place=place):
                shape = (BLOCK, HD)
                return chunk[place, :, 0].reshape(shape), chunk[place, :, 1].reshape(shape)

            owner = (first + place) * 8 + from_x * 2 + from_core
            loads.append((hits_ref[inst, req, owner] >= 0, rows))

    begin()
    top_ref[...] = high_ref[...]
    count = gather(loads, keys_ref, values_ref)
    sweep(count, (8, 4, 2, 1), keys_ref, values_ref, quick_step, state + (top_ref,))

    @pl.when(jnp.max(top_ref[...] - high_ref[...]) > MARGIN)
    def _():
        begin()
        sweep(count, (2, 1), keys_ref, values_ref, step, state)

    if last:
        for head in range(out_ref.shape[1] // HD):
            cols = slice(head * HD, (head + 1) * HD)
            done = acc_ref[:, cols] / total_ref[:, cols]
            out_ref[:, cols] = done.T.astype(out_ref.dtype)


def attention(where, unit, given, chunks, opens=False, last=False):
    rows = given[0].shape[1]
    arrays = [chunk for chunk, _ in chunks]
    blocks = sum(array.shape[0] for array in arrays) + 16 * opens
    held = [
        jax.ShapeDtypeStruct((1, rows), jnp.float32),
        jax.ShapeDtypeStruct((1, rows), jnp.float32),
        jax.ShapeDtypeStruct((HD, rows), jnp.float32),
    ]
    turned = [jax.ShapeDtypeStruct((HD, rows), jnp.bfloat16)] * opens
    out_shape = turned + held
    scratch = []
    if last:
        out_shape = turned + [jax.ShapeDtypeStruct((BLOCK, rows), jnp.bfloat16)]
        scratch = [pltpu.VMEM(one.shape, one.dtype) for one in held]
    scratch += [pltpu.VMEM((blocks * BLOCK, HD), jnp.bfloat16)] * 2
    scratch += [pltpu.VMEM((1, rows), jnp.float32)]
    return pl.pallas_call(
        functools.partial(attention_kernel, unit, opens, [origin for _, origin in chunks], last),
        in_specs=[SMEM] * 3 + [VMEM] * (len(given) + len(arrays)),
        out_specs=[VMEM] * len(out_shape),
        out_shape=out_shape,
        scratch_shapes=scratch,
        compiler_params=pltpu.CompilerParams(vmem_limit_bytes=VMEM_LIMIT),
        cost_estimate=pl.CostEstimate(
            flops=4 * blocks * BLOCK * HD * rows, bytes_accessed=2 << 20, transcendentals=0
        ),
        name=f"attention_{unit}{'_first' * opens}{'_last' * last}",
    )(*where, *given, *arrays)


def write_kernel(coords_ref, slot_ref, pool_ref, *refs):
    pieces, out_ref = refs[:-1], refs[-1]
    out_ref[...] = pool_ref[...]
    held = pool_ref.shape[0]
    slot = slot_ref[0, 0]

    @pl.when(slot // held == pl.program_id(0))
    def _():
        for back, piece in enumerate(pieces):
            width = piece.shape[2]
            source = lax.rem(coords_ref[4] - back + 4, 4)
            cols = pl.ds(pl.multiple_of(source * width, width), width)
            out_ref[lax.rem(slot, held), :, :, cols] = piece[...]


def write_block(coords, slots, pool, pieces):
    count = pool.shape[0]
    steps = 4
    blocked = pl.BlockSpec((count // steps,) + pool.shape[1:], lambda i: (i, 0, 0, 0))
    return pl.pallas_call(
        write_kernel,
        grid=(steps,),
        in_specs=[SMEM, SMEM, blocked] + [VMEM] * len(pieces),
        out_specs=blocked,
        out_shape=jax.ShapeDtypeStruct(pool.shape, pool.dtype),
        cost_estimate=pl.CostEstimate(flops=0, bytes_accessed=4 * pool.size, transcendentals=0),
        name="write_block",
    )(coords, slots, pool, *pieces)


def halves(array, side, axis):
    first, second = jnp.split(array, 2, axis=axis)
    return jnp.where(side == 0, first, second), jnp.where(side == 0, second, first)


def local(queries, suffix_kv, pool, hits, lengths, write_slot):
    names = ("inst", "zh", "x", "core", "tp")
    coords = jnp.stack([lax.axis_index(name) for name in names]).astype(jnp.int32)
    zh = lax.axis_index("zh")
    part_rows = pool.shape[2]

    suffix_mine, suffix_sent = halves(suffix_kv, zh, 2)
    suffix_other = shifted(jnp.concatenate([suffix_sent[0], suffix_sent[1]], axis=1), "zh", 1)
    written = shifted(suffix_kv, "inst", 1)

    sent = pick_blocks(coords, hits, pool).reshape(32, 2, part_rows, HD)
    sent, suffix_other, written, queries = lax.optimization_barrier(
        (sent, suffix_other, written, queries)
    )
    fetched = lax.all_to_all(sent, ("inst", "zh", "tp"), split_axis=0, concat_axis=0, tiled=True)
    own = fetched.reshape(8, 4, 2, part_rows, HD)

    query_mine, query_sent = halves(queries, zh, 1)
    query_other = shifted(query_sent, "zh", 1)
    suffix_mine = jnp.concatenate([suffix_mine[0], suffix_mine[1]], axis=1)
    near = jnp.stack([suffix_mine, suffix_other])
    near = jnp.stack([near] + [shifted(near, "x", far) for far in (1, 2, 3)])
    far = shifted(near, "core", 1)
    where = (coords, lengths, hits)

    def both(chunk, back, first):
        return [(chunk, (back, False, first)), (shifted(chunk, "core", 1), (back, True, first))]

    left = shifted(own, "x", 1)
    right = shifted(own, "x", 3)
    opposite = shifted(left[:4], "x", 1)
    opposed = shifted(right[4:], "x", 3)
    start = both(own, 0, 0)
    sides = both(left, 1, 0) + both(right, 3, 0)
    ends = both(opposite, 2, 0) + both(opposed, 2, 4)

    held = attention(where, 0, (query_mine, near, far), start, opens=True)
    others = attention(where, 1, (query_other, near, far), start + sides, opens=True)
    for_other = attention(where, 1, others, ends, last=True)[0]
    theirs = shifted(for_other, "zh", 1)
    held, _ = lax.optimization_barrier((held, for_other))
    mine = attention(where, 0, held, sides + ends, last=True)[0]
    first = jnp.where(zh == 0, mine, theirs)
    second = jnp.where(zh == 0, theirs, mine)
    attended = jnp.concatenate([first, second], axis=1)

    written, _ = lax.optimization_barrier((written, left))
    turned = lax.dynamic_slice_in_dim(
        jnp.concatenate([written, written], axis=1),
        lax.axis_index("tp") * part_rows,
        written.shape[1],
        axis=1,
    )
    pieces = [turned[:, back * part_rows : (back + 1) * part_rows] for back in range(4)]
    pieces = [shifted(piece, "tp", back) if back else piece for back, piece in enumerate(pieces)]
    pieces, _ = lax.optimization_barrier((pieces, mine))
    new_pool = write_block(coords, write_slot, pool, pieces)
    return attended, new_pool


def solution(mesh):
    split = Mesh(mesh.devices.reshape(4, 2, 4, 2, 4), ("inst", "zh", "x", "core", "tp"))
    ctx = ("inst", "zh", "x", "core")
    placed = (
        P(ctx, "tp"),
        P(None, ctx, "tp"),
        P(ctx, None, "tp", None),
        P(),
        P(),
        P(ctx, None),
    )
    return jax.shard_map(
        local,
        mesh=split,
        in_specs=placed,
        out_specs=(P(ctx, "tp"), P(ctx, None, "tp", None)),
        check_vma=False,
    )
```

```python
import functools
import math

import jax
import jax.numpy as jnp
from jax import lax
from jax.experimental import pallas as pl
from jax.experimental.pallas import tpu as pltpu
from jax.sharding import Mesh, PartitionSpec as P

HD = 128
BLOCK = 128
NEG = -1e30
MARGIN = 64.0
SCALE = HD ** -0.5 * math.log2(math.e)
VMEM_LIMIT = 16 * 1024 * 1024
SMEM = pl.BlockSpec(memory_space=pltpu.SMEM)
VMEM = pl.BlockSpec(memory_space=pltpu.VMEM)


def shifted(block, axis, distance):
    count = lax.axis_size(axis)
    return lax.ppermute(block, axis, [(i, (i + distance) % count) for i in range(count)])


def pick_kernel(coords_ref, hits_ref, pool_ref, out_ref, blocks_ref, sems):
    insts, zh, x, core = hits_ref.shape[1], coords_ref[1], coords_ref[2], coords_ref[3]
    owner = ((coords_ref[0] * 2 + zh) * 4 + x) * 2 + core
    copies = []
    for inst in range(insts):
        block = hits_ref[0, inst, owner]
        for req in range(1, hits_ref.shape[0]):
            block = jnp.maximum(block, hits_ref[req, inst, owner])
        slot = block - owner * pool_ref.shape[0]
        copies.append(
            pltpu.make_async_copy(pool_ref.at[slot], blocks_ref.at[inst], sems.at[inst])
        )
    for copy in copies:
        copy.start()
    for inst, copy in enumerate(copies):
        copy.wait()
        for part in range(8):
            out_ref[inst, part % 2, part // 2] = blocks_ref[
                inst, :, :, part * HD : (part + 1) * HD
            ]


def pick_blocks(coords, hits, pool):
    insts = hits.shape[1]
    _, two, rows, cols = pool.shape
    return pl.pallas_call(
        pick_kernel,
        in_specs=[SMEM, SMEM, pl.BlockSpec(memory_space=pl.ANY)],
        out_specs=VMEM,
        out_shape=jax.ShapeDtypeStruct((insts, 2, 4, two, rows, HD), pool.dtype),
        scratch_shapes=[
            pltpu.VMEM((insts, two, rows, cols), pool.dtype),
            pltpu.SemaphoreType.DMA((insts,)),
        ],
        name="pick_blocks",
    )(coords, hits, pool)


def scored(keys, queries_ref):
    return SCALE * jnp.dot(keys, queries_ref[...], preferred_element_type=jnp.float32)


def weighed(values, weights):
    return jnp.dot(values.T, weights.astype(jnp.bfloat16), preferred_element_type=jnp.float32)


def first_step(keys, values, queries_ref, high_ref, total_ref, acc_ref):
    scores = scored(keys, queries_ref)
    key_at = lax.broadcasted_iota(jnp.int32, scores.shape, 0)
    query_at = lax.rem(lax.broadcasted_iota(jnp.int32, scores.shape, 1), BLOCK)
    scores = jnp.where(key_at <= query_at, scores, NEG)
    high = jnp.max(scores, axis=0, keepdims=True)
    weights = jnp.exp2(scores - high)
    high_ref[...] = high
    total_ref[...] = jnp.sum(weights, axis=0, keepdims=True)
    acc_ref[...] = weighed(values, weights)


def step(keys, values, queries_ref, high_ref, total_ref, acc_ref):
    scores = scored(keys, queries_ref)
    before = high_ref[...]
    high = jnp.maximum(before, jnp.max(scores, axis=0, keepdims=True))
    faded = jnp.exp2(before - high)
    weights = jnp.exp2(scores - high)
    high_ref[...] = high
    total_ref[...] = total_ref[...] * faded + jnp.sum(weights, axis=0, keepdims=True)
    acc_ref[...] = acc_ref[...] * faded + weighed(values, weights)


def quick_step(keys, values, queries_ref, high_ref, total_ref, acc_ref, top_ref):
    scores = scored(keys, queries_ref)
    top_ref[...] = jnp.maximum(top_ref[...], jnp.max(scores, axis=0, keepdims=True))
    weights = jnp.exp2(scores - high_ref[...])
    total_ref[...] += jnp.sum(weights, axis=0, keepdims=True)
    acc_ref[...] += weighed(values, weights)


def gather(loads, keys_ref, values_ref):
    count = jnp.int32(0)
    for wanted, load in loads:

        @pl.when(wanted)
        def _(count=count, load=load):
            keys, values = load()
            span = pl.ds(pl.multiple_of(count * BLOCK, BLOCK), BLOCK)
            keys_ref[span, :] = keys
            values_ref[span, :] = values

        count = count + wanted.astype(jnp.int32)
    return count


def sweep(count, widths, keys_ref, values_ref, one_step, state):
    def many(first, blocks):
        span = pl.ds(pl.multiple_of(first * BLOCK, BLOCK), blocks * BLOCK)
        one_step(keys_ref[span, :], values_ref[span, :], *state)

    widest = widths[0]

    def turn(index, carry):
        many(index * widest, widest)
        return carry

    lax.fori_loop(0, count // widest, turn, 0)
    done = count // widest * widest
    for width in widths[1:]:
        fits = count - done >= width
        pl.when(fits)(functools.partial(many, done, width))
        done = done + jnp.where(fits, width, 0)


def request_at(lengths_ref, inst, place):
    first = lengths_ref[inst, 0]
    second = first + lengths_ref[inst, 1]
    third = second + lengths_ref[inst, 2]
    return sum((place >= edge).astype(jnp.int32) for edge in (first, second, third))


def attention_kernel(unit, opens, origins, last, coords_ref, lengths_ref, hits_ref, *refs):
    given, refs = refs[: 3 if opens else 4], refs[3 if opens else 4 :]
    chunks, refs = refs[: len(origins)], refs[len(origins) :]
    if opens:
        query_ref, near_ref, far_ref = given
        queries_ref, refs = refs[0], refs[1:]
    else:
        queries_ref, high_in, total_in, acc_in = given
    if last:
        out_ref, refs = refs[0], refs[1:]
    high_ref, total_ref, acc_ref, keys_ref, values_ref, top_ref = refs
    state = (queries_ref, high_ref, total_ref, acc_ref)
    inst, zh, x, core = (coords_ref[i] for i in range(4))
    here = ((1 - zh if unit else zh) * 4 + x) * 2 + core
    req = request_at(lengths_ref, inst, here)
    loads = []

    if opens:
        for head in range(queries_ref.shape[1] // HD):
            cols = slice(head * HD, (head + 1) * HD)
            queries_ref[:, cols] = query_ref[:, cols].T
        for turned, source in enumerate((near_ref, far_ref)):
            for back in range(4):
                for side in range(2):
                    from_zh = 1 - zh if side else zh
                    from_core = 1 - core if turned else core
                    place = (from_zh * 4 + lax.rem(x - back + 4, 4)) * 2 + from_core
                    wanted = (place < here) & (request_at(lengths_ref, inst, place) == req)
                    rows = (lambda s=source, b=back, h=side: (s[b, h, :, :HD], s[b, h, :, HD:]))
                    loads.append((wanted, rows))

        def begin():
            first_step(near_ref[0, unit, :, :HD], near_ref[0, unit, :, HD:], *state)

    else:

        def begin():
            high_ref[...] = high_in[...]
            total_ref[...] = total_in[...]
            acc_ref[...] = acc_in[...]

    for chunk, (back, turned, first) in zip(chunks, origins):
        from_x = lax.rem(x - back + 4, 4)
        from_core = 1 - core if turned else core
        for place in range(chunk.shape[0]):

            def rows(chunk=chunk, place=place):
                shape = (BLOCK, HD)
                return chunk[place, :, 0].reshape(shape), chunk[place, :, 1].reshape(shape)

            owner = (first + place) * 8 + from_x * 2 + from_core
            loads.append((hits_ref[req, inst, owner] >= 0, rows))

    begin()
    top_ref[...] = high_ref[...]
    count = gather(loads, keys_ref, values_ref)
    sweep(count, (8, 4, 2, 1), keys_ref, values_ref, quick_step, state + (top_ref,))

    @pl.when(jnp.max(top_ref[...] - high_ref[...]) > MARGIN)
    def _():
        begin()
        sweep(count, (2, 1), keys_ref, values_ref, step, state)

    if last:
        for head in range(out_ref.shape[1] // HD):
            cols = slice(head * HD, (head + 1) * HD)
            done = acc_ref[:, cols] / total_ref[:, cols]
            out_ref[:, cols] = done.T.astype(out_ref.dtype)


def attention(where, unit, given, chunks, opens=False, last=False):
    rows = given[0].shape[1]
    arrays = [chunk for chunk, _ in chunks]
    blocks = sum(array.shape[0] for array in arrays) + 16 * opens
    held = [
        jax.ShapeDtypeStruct((1, rows), jnp.float32),
        jax.ShapeDtypeStruct((1, rows), jnp.float32),
        jax.ShapeDtypeStruct((HD, rows), jnp.float32),
    ]
    turned = [jax.ShapeDtypeStruct((HD, rows), jnp.bfloat16)] * opens
    out_shape = turned + held
    scratch = []
    if last:
        out_shape = turned + [jax.ShapeDtypeStruct((BLOCK, rows), jnp.bfloat16)]
        scratch = [pltpu.VMEM(one.shape, one.dtype) for one in held]
    scratch += [pltpu.VMEM((blocks * BLOCK, HD), jnp.bfloat16)] * 2
    scratch += [pltpu.VMEM((1, rows), jnp.float32)]
    return pl.pallas_call(
        functools.partial(attention_kernel, unit, opens, [origin for _, origin in chunks], last),
        in_specs=[SMEM] * 3 + [VMEM] * (len(given) + len(arrays)),
        out_specs=[VMEM] * len(out_shape),
        out_shape=out_shape,
        scratch_shapes=scratch,
        compiler_params=pltpu.CompilerParams(vmem_limit_bytes=VMEM_LIMIT),
        cost_estimate=pl.CostEstimate(
            flops=40 * blocks * BLOCK * HD * rows, bytes_accessed=2 << 20, transcendentals=0
        ),
        name=f"attention_{unit}{'_first' * opens}{'_last' * last}",
    )(*where, *given, *arrays)


def copy_kernel(pool_ref, out_ref):
    out_ref[...] = pool_ref[...]


def copy_pool(pool):
    steps = 4
    blocked = pl.BlockSpec((pool.shape[0] // steps,) + pool.shape[1:], lambda i: (i, 0, 0, 0))
    return pl.pallas_call(
        copy_kernel,
        grid=(steps,),
        in_specs=[blocked],
        out_specs=blocked,
        out_shape=jax.ShapeDtypeStruct(pool.shape, pool.dtype),
        cost_estimate=pl.CostEstimate(flops=0, bytes_accessed=4 * pool.size, transcendentals=0),
        name="copy_pool",
    )(pool)


def write_kernel(coords_ref, slot_ref, pool_ref, *refs):
    pieces, out_ref, block_ref, sem = refs[:-3], refs[-3], refs[-2], refs[-1]
    for back, piece in enumerate(pieces):
        width = piece.shape[2]
        source = lax.rem(coords_ref[4] - back + 4, 4)
        cols = pl.ds(pl.multiple_of(source * width, width), width)
        block_ref[:, :, cols] = piece[...]
    copy = pltpu.make_async_copy(block_ref, out_ref.at[slot_ref[0, 0]], sem)
    copy.start()
    copy.wait()


def write_block(coords, slots, pool, pieces):
    anywhere = pl.BlockSpec(memory_space=pl.ANY)
    return pl.pallas_call(
        write_kernel,
        in_specs=[SMEM, SMEM, anywhere] + [VMEM] * len(pieces),
        out_specs=anywhere,
        out_shape=jax.ShapeDtypeStruct(pool.shape, pool.dtype),
        scratch_shapes=[pltpu.VMEM(pool.shape[1:], pool.dtype), pltpu.SemaphoreType.DMA],
        input_output_aliases={2: 0},
        name="write_block",
    )(coords, slots, pool, *pieces)


def halves(array, side, axis):
    first, second = jnp.split(array, 2, axis=axis)
    return jnp.where(side == 0, first, second), jnp.where(side == 0, second, first)


def local(queries, suffix_kv, pool, hits, lengths, write_slot):
    names = ("inst", "zh", "x", "core", "tp")
    coords = jnp.stack([lax.axis_index(name) for name in names]).astype(jnp.int32)
    hits = jnp.transpose(hits, (1, 0, 2))
    zh = lax.axis_index("zh")
    part_rows = pool.shape[2]

    suffix_mine, suffix_sent = halves(suffix_kv, zh, 2)
    suffix_other = shifted(jnp.concatenate([suffix_sent[0], suffix_sent[1]], axis=1), "zh", 1)
    written = shifted(suffix_kv, "inst", 1)

    sent = pick_blocks(coords, hits, pool).reshape(32, 2, part_rows, HD)
    sent, suffix_other, written, queries = lax.optimization_barrier(
        (sent, suffix_other, written, queries)
    )
    fetched = lax.all_to_all(sent, ("inst", "zh", "tp"), split_axis=0, concat_axis=0, tiled=True)

    query_mine, query_sent = halves(queries, zh, 1)
    suffix_mine = jnp.concatenate([suffix_mine[0], suffix_mine[1]], axis=1)
    near = jnp.stack([suffix_mine, suffix_other])
    near = jnp.stack([near] + [shifted(near, "x", far) for far in (1, 2, 3)])
    far = shifted(near, "core", 1)
    copied = copy_pool(pool)
    fetched, query_sent, copied = lax.optimization_barrier((fetched, query_sent, copied))
    own = fetched.reshape(8, 4, 2, part_rows, HD)
    query_other = shifted(query_sent, "zh", 1)

    where = (coords, lengths, hits)

    def both(chunk, back, first):
        return [(chunk, (back, False, first)), (shifted(chunk, "core", 1), (back, True, first))]

    left = shifted(own, "x", 1)
    right = shifted(own, "x", 3)
    opposite = shifted(left[:4], "x", 1)
    opposed = shifted(right[4:], "x", 3)
    start = both(own, 0, 0)
    sides = both(left, 1, 0) + both(right, 3, 0)
    ends = both(opposite, 2, 0) + both(opposed, 2, 4)

    held = attention(where, 0, (query_mine, near, far), start, opens=True)
    others = attention(where, 1, (query_other, near, far), start + sides, opens=True)
    for_other = attention(where, 1, others, ends, last=True)[0]
    theirs = shifted(for_other, "zh", 1)
    held, _ = lax.optimization_barrier((held, for_other))
    mine = attention(where, 0, held, sides + ends, last=True)[0]
    first = jnp.where(zh == 0, mine, theirs)
    second = jnp.where(zh == 0, theirs, mine)
    attended = jnp.concatenate([first, second], axis=1)

    written, _ = lax.optimization_barrier((written, for_other))
    turned = lax.dynamic_slice_in_dim(
        jnp.concatenate([written, written], axis=1),
        lax.axis_index("tp") * part_rows,
        written.shape[1],
        axis=1,
    )
    pieces = [turned[:, back * part_rows : (back + 1) * part_rows] for back in range(4)]
    pieces = [shifted(piece, "tp", back) if back else piece for back, piece in enumerate(pieces)]
    pieces, copied, _ = lax.optimization_barrier((pieces, copied, mine))
    new_pool = write_block(coords, write_slot, copied, pieces)
    return attended, new_pool


def solution(mesh):
    split = Mesh(mesh.devices.reshape(4, 2, 4, 2, 4), ("inst", "zh", "x", "core", "tp"))
    ctx = ("inst", "zh", "x", "core")
    placed = (
        P(ctx, "tp"),
        P(None, ctx, "tp"),
        P(ctx, None, "tp", None),
        P(),
        P(),
        P(ctx, None),
    )
    return jax.shard_map(
        local,
        mesh=split,
        in_specs=placed,
        out_specs=(P(ctx, "tp"), P(ctx, None, "tp", None)),
        check_vma=False,
    )
```

```python
import functools
import math

import jax
import jax.numpy as jnp
from jax import lax
from jax.experimental import pallas as pl
from jax.experimental.pallas import tpu as pltpu
from jax.sharding import Mesh, PartitionSpec as P

HD = 128
BLOCK = 128
NEG = -1e30
LARGE = 2.0**64
NAMES = ("inst", "zh", "x", "core", "tp")
SCALE = HD ** -0.5 * math.log2(math.e)
VMEM_LIMIT = 16 * 1024 * 1024
SMEM = pl.BlockSpec(memory_space=pltpu.SMEM)
VMEM = pl.BlockSpec(memory_space=pltpu.VMEM)


def shifted(block, axis, distance):
    count = lax.axis_size(axis)
    return lax.ppermute(block, axis, [(i, (i + distance) % count) for i in range(count)])


def pick_kernel(hits_ref, pool_ref, out_ref, blocks_ref, sems):
    insts = hits_ref.shape[1]
    inst, zh, x, core = (lax.axis_index(name) for name in NAMES[:4])
    owner = ((inst * 2 + zh) * 4 + x) * 2 + core
    copies = []
    for inst in range(insts):
        block = hits_ref[0, inst, owner]
        for req in range(1, hits_ref.shape[0]):
            block = jnp.maximum(block, hits_ref[req, inst, owner])
        slot = block - owner * pool_ref.shape[0]
        copies.append(
            pltpu.make_async_copy(pool_ref.at[slot], blocks_ref.at[inst], sems.at[inst])
        )
    for copy in copies:
        copy.start()
    for inst, copy in enumerate(copies):
        copy.wait()
        for part in range(8):
            out_ref[inst, part % 2, part // 2] = blocks_ref[
                inst, :, :, part * HD : (part + 1) * HD
            ]


def pick_blocks(hits, pool):
    insts = hits.shape[1]
    _, two, rows, cols = pool.shape
    return pl.pallas_call(
        pick_kernel,
        in_specs=[SMEM, pl.BlockSpec(memory_space=pl.ANY)],
        out_specs=VMEM,
        out_shape=jax.ShapeDtypeStruct((insts, 2, 4, two, rows, HD), pool.dtype),
        scratch_shapes=[
            pltpu.VMEM((insts, two, rows, cols), pool.dtype),
            pltpu.SemaphoreType.DMA((insts,)),
        ],
        name="pick_blocks",
    )(hits, pool)


def scored(keys, queries_ref):
    return SCALE * jnp.dot(keys, queries_ref[...], preferred_element_type=jnp.float32)


def weighed(values, weights):
    return jnp.dot(values.T, weights.astype(jnp.bfloat16), preferred_element_type=jnp.float32)


def first_step(keys, values, queries_ref, high_ref, total_ref, acc_ref):
    scores = scored(keys, queries_ref)
    key_at = lax.broadcasted_iota(jnp.int32, scores.shape, 0)
    query_at = lax.rem(lax.broadcasted_iota(jnp.int32, scores.shape, 1), BLOCK)
    scores = jnp.where(key_at <= query_at, scores, NEG)
    high = jnp.max(scores, axis=0, keepdims=True)
    weights = jnp.exp2(scores - high)
    high_ref[...] = high
    total_ref[...] = jnp.sum(weights, axis=0, keepdims=True)
    acc_ref[...] = weighed(values, weights)


def step(keys, values, queries_ref, high_ref, total_ref, acc_ref):
    scores = scored(keys, queries_ref)
    before = high_ref[...]
    high = jnp.maximum(before, jnp.max(scores, axis=0, keepdims=True))
    faded = jnp.exp2(before - high)
    weights = jnp.exp2(scores - high)
    high_ref[...] = high
    total_ref[...] = total_ref[...] * faded + jnp.sum(weights, axis=0, keepdims=True)
    acc_ref[...] = acc_ref[...] * faded + weighed(values, weights)


def quick_step(keys, values, queries_ref, high_ref, total_ref, acc_ref):
    weights = jnp.exp2(scored(keys, queries_ref) - high_ref[...])
    total_ref[...] += jnp.sum(weights, axis=0, keepdims=True)
    acc_ref[...] += weighed(values, weights)


def gather(loads, keys_ref, values_ref):
    count = jnp.int32(0)
    for wanted, load in loads:

        @pl.when(wanted)
        def _(count=count, load=load):
            keys, values = load()
            span = pl.ds(pl.multiple_of(count * BLOCK, BLOCK), BLOCK)
            keys_ref[span, :] = keys
            values_ref[span, :] = values

        count = count + wanted.astype(jnp.int32)
    return count


def sweep(count, widths, keys_ref, values_ref, one_step, state):
    def many(first, blocks):
        span = pl.ds(pl.multiple_of(first * BLOCK, BLOCK), blocks * BLOCK)
        one_step(keys_ref[span, :], values_ref[span, :], *state)

    widest = widths[0]

    def turn(index, carry):
        many(index * widest, widest)
        return carry

    lax.fori_loop(0, count // widest, turn, 0)
    done = count // widest * widest
    for width in widths[1:]:
        fits = count - done >= width
        pl.when(fits)(functools.partial(many, done, width))
        done = done + jnp.where(fits, width, 0)


def request_at(lengths_ref, inst, place):
    first = lengths_ref[inst, 0]
    second = first + lengths_ref[inst, 1]
    third = second + lengths_ref[inst, 2]
    return sum((place >= edge).astype(jnp.int32) for edge in (first, second, third))


def attention_kernel(unit, opens, origins, last, lengths_ref, hits_ref, *refs):
    given, refs = refs[: 3 if opens else 4], refs[3 if opens else 4 :]
    chunks, refs = refs[: len(origins)], refs[len(origins) :]
    if opens:
        query_ref, near_ref, far_ref = given
        queries_ref, refs = refs[0], refs[1:]
    else:
        queries_ref, high_in, total_in, acc_in = given
    if last:
        out_ref, refs = refs[0], refs[1:]
    high_ref, total_ref, acc_ref, keys_ref, values_ref = refs
    state = (queries_ref, high_ref, total_ref, acc_ref)
    inst, zh, x, core = (lax.axis_index(name) for name in NAMES[:4])
    here = ((1 - zh if unit else zh) * 4 + x) * 2 + core
    req = request_at(lengths_ref, inst, here)
    loads = []

    if opens:
        for head in range(queries_ref.shape[1] // HD):
            cols = slice(head * HD, (head + 1) * HD)
            queries_ref[:, cols] = query_ref[:, cols].T
        for turned, source in enumerate((near_ref, far_ref)):
            for back in range(4):
                for side in range(2):
                    from_zh = 1 - zh if side else zh
                    from_core = 1 - core if turned else core
                    place = (from_zh * 4 + lax.rem(x - back + 4, 4)) * 2 + from_core
                    wanted = (place < here) & (request_at(lengths_ref, inst, place) == req)
                    rows = (lambda s=source, b=back, h=side: (s[b, h, :, :HD], s[b, h, :, HD:]))
                    loads.append((wanted, rows))

        def begin():
            first_step(near_ref[0, unit, :, :HD], near_ref[0, unit, :, HD:], *state)

    else:

        def begin():
            high_ref[...] = high_in[...]
            total_ref[...] = total_in[...]
            acc_ref[...] = acc_in[...]

    for chunk, (back, turned, first) in zip(chunks, origins):
        from_x = lax.rem(x - back + 4, 4)
        from_core = 1 - core if turned else core
        for place in range(chunk.shape[0]):

            def rows(chunk=chunk, place=place):
                shape = (BLOCK, HD)
                return chunk[place, :, 0].reshape(shape), chunk[place, :, 1].reshape(shape)

            owner = (first + place) * 8 + from_x * 2 + from_core
            loads.append((hits_ref[req, inst, owner] >= 0, rows))

    begin()
    count = gather(loads, keys_ref, values_ref)
    sweep(count, (8, 4, 3, 2, 1), keys_ref, values_ref, quick_step, state)

    @pl.when(jnp.max(total_ref[...]) > LARGE)
    def _():
        begin()
        sweep(count, (2, 1), keys_ref, values_ref, step, state)

    if last:
        done = (acc_ref[...] * (1.0 / total_ref[...])).astype(out_ref.dtype)
        for head in range(out_ref.shape[1] // HD):
            cols = slice(head * HD, (head + 1) * HD)
            out_ref[:, cols] = done[:, cols].T


def attention(where, unit, given, chunks, opens=False, last=False):
    rows = given[0].shape[1]
    arrays = [chunk for chunk, _ in chunks]
    blocks = sum(array.shape[0] for array in arrays) + 16 * opens
    held = [
        jax.ShapeDtypeStruct((1, rows), jnp.float32),
        jax.ShapeDtypeStruct((1, rows), jnp.float32),
        jax.ShapeDtypeStruct((HD, rows), jnp.float32),
    ]
    turned = [jax.ShapeDtypeStruct((HD, rows), jnp.bfloat16)] * opens
    out_shape = turned + held
    scratch = []
    if last:
        out_shape = turned + [jax.ShapeDtypeStruct((BLOCK, rows), jnp.bfloat16)]
        scratch = [pltpu.VMEM(one.shape, one.dtype) for one in held]
    scratch += [pltpu.VMEM((blocks * BLOCK, HD), jnp.bfloat16)] * 2
    return pl.pallas_call(
        functools.partial(attention_kernel, unit, opens, [origin for _, origin in chunks], last),
        in_specs=[SMEM] * 2 + [VMEM] * (len(given) + len(arrays)),
        out_specs=[VMEM] * len(out_shape),
        out_shape=out_shape,
        scratch_shapes=scratch,
        compiler_params=pltpu.CompilerParams(vmem_limit_bytes=VMEM_LIMIT),
        cost_estimate=pl.CostEstimate(
            flops=40 * blocks * BLOCK * HD * rows, bytes_accessed=2 << 20, transcendentals=0
        ),
        name=f"attention_{unit}{'_first' * opens}{'_last' * last}",
    )(*where, *given, *arrays)


def copy_kernel(pool_ref, out_ref):
    out_ref[...] = pool_ref[...]


def copy_pool(pool):
    steps = 4
    blocked = pl.BlockSpec((pool.shape[0] // steps,) + pool.shape[1:], lambda i: (i, 0, 0, 0))
    return pl.pallas_call(
        copy_kernel,
        grid=(steps,),
        in_specs=[blocked],
        out_specs=blocked,
        out_shape=jax.ShapeDtypeStruct(pool.shape, pool.dtype),
        cost_estimate=pl.CostEstimate(flops=0, bytes_accessed=4 * pool.size, transcendentals=0),
        name="copy_pool",
    )(pool)


def write_kernel(slot_ref, pool_ref, *refs):
    pieces, out_ref, block_ref, sem = refs[:-3], refs[-3], refs[-2], refs[-1]
    for back, piece in enumerate(pieces):
        width = piece.shape[2]
        source = lax.rem(lax.axis_index("tp") - back + 4, 4)
        cols = pl.ds(pl.multiple_of(source * width, width), width)
        block_ref[:, :, cols] = piece[...]
    copy = pltpu.make_async_copy(block_ref, out_ref.at[slot_ref[0, 0]], sem)
    copy.start()
    copy.wait()


def write_block(slots, pool, pieces):
    anywhere = pl.BlockSpec(memory_space=pl.ANY)
    return pl.pallas_call(
        write_kernel,
        in_specs=[SMEM, anywhere] + [VMEM] * len(pieces),
        out_specs=anywhere,
        out_shape=jax.ShapeDtypeStruct(pool.shape, pool.dtype),
        scratch_shapes=[pltpu.VMEM(pool.shape[1:], pool.dtype), pltpu.SemaphoreType.DMA],
        input_output_aliases={1: 0},
        name="write_block",
    )(slots, pool, *pieces)


def halves(array, side, axis):
    first, second = jnp.split(array, 2, axis=axis)
    return jnp.where(side == 0, first, second), jnp.where(side == 0, second, first)


def local(queries, suffix_kv, pool, hits, lengths, write_slot):
    hits = jnp.transpose(hits, (1, 0, 2))
    zh = lax.axis_index("zh")
    part_rows = pool.shape[2]

    suffix_mine, suffix_sent = halves(suffix_kv, zh, 2)
    suffix_sent = jnp.concatenate([suffix_sent[0], suffix_sent[1]], axis=1)
    written, suffix_sent = lax.optimization_barrier((suffix_kv, suffix_sent))
    suffix_other = shifted(suffix_sent, "zh", 1)
    written = shifted(written, "inst", 1)

    sent = pick_blocks(hits, pool).reshape(32, 2, part_rows, HD)
    sent, suffix_other, written, queries = lax.optimization_barrier(
        (sent, suffix_other, written, queries)
    )
    fetched = lax.all_to_all(sent, ("inst", "zh", "tp"), split_axis=0, concat_axis=0, tiled=True)

    query_mine, query_sent = halves(queries, zh, 1)
    suffix_mine = jnp.concatenate([suffix_mine[0], suffix_mine[1]], axis=1)
    near = jnp.stack([suffix_mine, suffix_other])
    near = jnp.stack([near] + [shifted(near, "x", far) for far in (1, 2, 3)])
    far = shifted(near, "core", 1)
    copied = copy_pool(pool)
    fetched, query_sent, copied = lax.optimization_barrier((fetched, query_sent, copied))
    own = fetched.reshape(8, 4, 2, part_rows, HD)
    query_other = shifted(query_sent, "zh", 1)

    where = (lengths, hits)

    def both(chunk, back, first):
        return [(chunk, (back, False, first)), (shifted(chunk, "core", 1), (back, True, first))]

    left = shifted(own, "x", 1)
    right = shifted(own, "x", 3)
    opposite = shifted(left[:4], "x", 1)
    opposed = shifted(right[4:], "x", 3)
    start = both(own, 0, 0)
    sides = both(left, 1, 0) + both(right, 3, 0)
    ends = both(opposite, 2, 0) + both(opposed, 2, 4)

    held = attention(where, 0, (query_mine, near, far), start, opens=True)
    others = attention(where, 1, (query_other, near, far), start + sides, opens=True)
    for_other = attention(where, 1, others, ends, last=True)[0]
    theirs = shifted(for_other, "zh", 1)
    held, _ = lax.optimization_barrier((held, for_other))
    mine = attention(where, 0, held, sides + ends, last=True)[0]
    first = jnp.where(zh == 0, mine, theirs)
    second = jnp.where(zh == 0, theirs, mine)
    attended = jnp.concatenate([first, second], axis=1)

    written, _ = lax.optimization_barrier((written, for_other))
    turned = lax.dynamic_slice_in_dim(
        jnp.concatenate([written, written], axis=1),
        lax.axis_index("tp") * part_rows,
        written.shape[1],
        axis=1,
    )
    pieces = [turned[:, back * part_rows : (back + 1) * part_rows] for back in range(4)]
    pieces = [shifted(piece, "tp", back) if back else piece for back, piece in enumerate(pieces)]
    pieces, copied, _ = lax.optimization_barrier((pieces, copied, mine))
    new_pool = write_block(write_slot, copied, pieces)
    return attended, new_pool


def solution(mesh):
    split = Mesh(mesh.devices.reshape(4, 2, 4, 2, 4), ("inst", "zh", "x", "core", "tp"))
    ctx = ("inst", "zh", "x", "core")
    placed = (
        P(ctx, "tp"),
        P(None, ctx, "tp"),
        P(ctx, None, "tp", None),
        P(),
        P(),
        P(ctx, None),
    )
    return jax.shard_map(
        local,
        mesh=split,
        in_specs=placed,
        out_specs=(P(ctx, "tp"), P(ctx, None, "tp", None)),
        check_vma=False,
    )
```
